128 devices in a mesh: ctx: 64 (over x, y, z_hi, core), tp: 2 (over z_lo).
Axes of the slice: x: 4, y: 4, z: 4 (z_hi: 2, z_lo: 2; z = z_hi * 2 + z_lo), core: 2. Of those that a mesh axis runs over, the one named last changes fastest.
Arguments:
- queries: bfloat16 [16384, 4096], P(('ctx', 'tp')), may hold values from -5 to 5
- keys: bfloat16 [16384, 512], P(('ctx', 'tp')), may hold values from -5 to 5
- values: bfloat16 [16384, 512], P(('ctx', 'tp')), may hold values from -6 to 6
- d_out: bfloat16 [16384, 4096], P(('ctx', 'tp')), may hold values from -6 to 6
- lengths: int32 [64], replicated, may hold values from 64 to 256, as said below
- ancestors: int32 [64, 7], P('ctx'), may hold values from 0 to 1, as said below
- rewards: float32 [64], P('ctx'), may hold values from -11 to 11
- pruned: int32 [64], P('ctx'), may hold values 0 or 1
- branch_group: int32 [64], P('ctx'), may hold values from 0 to 7
Outputs:
- attended: bfloat16 [16384, 4096], P(('ctx', 'tp'))
- grad_queries: bfloat16 [16384, 4096], P(('ctx', 'tp'))
- grad_keys: bfloat16 [16384, 512], P(('ctx', 'tp'))
- grad_values: bfloat16 [16384, 512], P(('ctx', 'tp'))
- advantage: float32 [64], P('ctx')
The draws below stay inside these ranges and needn't reach their ends.
Inputs may be any that keep to these rules, and one draw needn't show every extreme that they name: Segments form trees of 8 consecutive segments starting at multiples of 8; ancestors[s, o - 1] is 1 when segment s - o is an ancestor of segment s in its tree. The first segment of a tree is an ancestor of all others; every segment has at most two ancestors. `lengths`: the first segment of every tree is full.
All inputs are finite; a program needn't handle non-finite values. No bound on the sum of `pruned` on one device may be relied on, other than what follows from the above.
Results may differ from the reference program's by a relative error of at most 0.02.
Values may be sent and summed in bfloat16 or wider, within the bound.
A program may use at most 192 MiB of HBM per device.

```python
import jax
import jax.numpy as jnp
from jax import lax

H = 32
KVH = 4
HD = 128
TILE = 256
PATHS_PER_FOREST = 8
GROUPS = 8
SEGS = 64
TOKENS = 16384


def draw_queries(key, part):
    key = jax.random.fold_in(key, 11)
    return jnp.clip(jax.random.normal(key, (TOKENS, H * HD), jnp.float32), -4.0, 4.0).astype(jnp.bfloat16)


def draw_keys(key, part):
    key = jax.random.fold_in(key, 12)
    return jnp.clip(jax.random.normal(key, (TOKENS, KVH * HD), jnp.float32), -4.0, 4.0).astype(jnp.bfloat16)


def draw_rewards(key, part):
    key = jax.random.fold_in(key, 21)
    rising = 1.0 + 2.0 * jnp.arange(SEGS).astype(jnp.float32) / max(SEGS - 1, 1)
    return jnp.clip(jax.random.normal(key, (SEGS,), jnp.float32), -3.5, 3.5) * rising


def draw_lengths(key, part):
    key = jax.random.fold_in(key, 31)
    slots = jnp.arange(SEGS, dtype=jnp.int32)
    drawn = jax.random.randint(key, (SEGS,), TILE // 4, TILE + 1, dtype=jnp.int32)
    drawn = jnp.where(slots % PATHS_PER_FOREST == 0, TILE, drawn)
    return jnp.where(slots == 1, TILE // 4, drawn).astype(jnp.int32)


def draw_ancestors(key, part):
    key = jax.random.fold_in(key, 41)
    sampled_forests = SEGS // PATHS_PER_FOREST
    piece_locations = jnp.arange(PATHS_PER_FOREST, dtype=jnp.int32)
    depth = jnp.ones((sampled_forests, PATHS_PER_FOREST), jnp.int32)
    owned = jnp.zeros((sampled_forests, PATHS_PER_FOREST, PATHS_PER_FOREST), jnp.int32)
    for section in range(1, PATHS_PER_FOREST):
        key, first_key, later_lookup_panel = jax.random.split(key, 3)
        softmax_logit = jax.random.randint(first_key, (sampled_forests, PATHS_PER_FOREST), 0, 1000, dtype=jnp.int32) * PATHS_PER_FOREST + piece_locations[None, :]
        sibling_credit = jax.random.randint(later_lookup_panel, (sampled_forests,), 0, 1000, dtype=jnp.int32) * PATHS_PER_FOREST
        softmax_logit = softmax_logit + jnp.where(piece_locations[None, :] == 0, sibling_credit[:, None], 0)
        allowed = (piece_locations[None, :] < section) & (depth <= 2)
        softmax_logit = jnp.where(allowed, softmax_logit, -1)
        parent = jnp.argmax(softmax_logit, axis=1).astype(jnp.int32)
        choose = (piece_locations[None, :] == parent[:, None]).astype(jnp.int32)
        inherited = jnp.einsum('tj,tjk->tk', choose, owned)
        owned = owned.at[:, section, :].set(jnp.clip(inherited + choose, 0, 1))
        depth = depth.at[:, section].set(jnp.sum(choose * depth, 1) + 1)
    matrix_columns = []
    for offset in range(1, PATHS_PER_FOREST):
        entries = []
        for place in range(PATHS_PER_FOREST):
            if place >= offset:
                entries.append(owned[:, place, place - offset])
            else:
                entries.append(jnp.zeros((sampled_forests,), jnp.int32))
        matrix_columns.append(jnp.stack(entries, 1).reshape(SEGS))
    return jnp.stack(matrix_columns, 1).astype(jnp.int32)


def plant(result, key, least, largest):
    extent = result.shape
    spot = [jax.random.randint(jax.random.fold_in(key, axis), (), 0, extent[axis]) for axis in range(len(extent))]
    result = result.at[tuple(spot)].set(least)
    longest = extent.index(max(extent))
    spot[longest] = (spot[longest] + 1) % extent[longest]
    return result.at[tuple(spot)].set(largest)


def shard_levels(rng, dims, pieces, smallest, largest):
    def one(position, parts):
        steps = jax.random.uniform(jax.random.fold_in(jax.random.fold_in(rng, 6), position), (parts,), jnp.float32, smallest / len(pieces), largest / len(pieces))
        return jnp.repeat(jnp.exp(steps), dims[position] // parts).reshape((-1,) + (1,) * (len(dims) - position - 1))

    gain = one(*pieces[0])
    for cut in pieces[1:]:
        gain = gain * one(*cut)
    return gain


def centred(key, dims, scale, limit, pieces=(), held_as=jnp.bfloat16):
    values = jax.random.normal(key, dims, jnp.float32) * scale
    if len(pieces) > 0:
        values = shard_levels(key, dims, pieces, -0.22, 0.18) * values
    return jnp.clip(values, min=-limit, max=limit).astype(held_as)


def setup_inputs(seed: int = 0) -> dict:
    seeds = jax.random.split(jax.random.key(seed), 10)
    return {
        "queries": draw_queries(jax.random.fold_in(seeds[9], 71), 0),
        "keys": draw_keys(jax.random.fold_in(seeds[9], 71), 0),
        "values": centred(seeds[2], (TOKENS, KVH * HD), 1.0, 6.0, ((0, 128),)),
        "d_out": centred(seeds[3], (TOKENS, H * HD), 1.0, 6.0, ((0, 128),)),
        "lengths": draw_lengths(jax.random.fold_in(seeds[9], 71), 0),
        "ancestors": draw_ancestors(jax.random.fold_in(seeds[9], 71), 0),
        "rewards": draw_rewards(jax.random.fold_in(seeds[9], 71), 0),
        "pruned": plant((jax.random.randint(seeds[7], (SEGS,), 0, 4) < 1).astype(jnp.int32), jax.random.fold_in(seeds[7], 1), 0, 1),
        "branch_group": plant(jax.random.randint(seeds[8], (SEGS,), 0, GROUPS), jax.random.fold_in(seeds[8], 1), 0, GROUPS - 1).astype(jnp.int32),
    }


def group_terms(rewards, pruned, branch_group):
    living = 1.0 - pruned.astype(jnp.float32)
    member = (branch_group[:, None] == jnp.arange(GROUPS, dtype=jnp.int32)[None, :]).astype(jnp.float32) * living[:, None]
    return (lax.optimization_barrier(jnp.sum(member, 0)), lax.optimization_barrier(jnp.sum(member * rewards[:, None], 0)), lax.optimization_barrier(jnp.sum(member * (rewards * rewards)[:, None], 0)))

def renormalize(rewards, pruned, branch_group, members, reward_sum, square_sum):
    denominator = jnp.maximum(members, 1.0)
    average = reward_sum / denominator
    spread = jnp.sqrt(jnp.maximum(square_sum / denominator - average * average, 0.0))
    divisor = jnp.maximum(spread, 1.0)
    living = 1.0 - pruned.astype(jnp.float32)
    belongs = (branch_group[:, None] == jnp.arange(GROUPS, dtype=jnp.int32)[None, :]).astype(jnp.float32)
    return living * (rewards - lax.optimization_barrier(jnp.sum(belongs * average[None, :], 1))) / lax.optimization_barrier(jnp.sum(belongs * divisor[None, :], 1))

def reference(queries, keys, values, d_out, lengths, ancestors, rewards, pruned, branch_group):
    members, reward_sum, square_sum = group_terms(rewards, pruned, branch_group)
    advantage = renormalize(rewards, pruned, branch_group, members, reward_sum, square_sum)
    group = H // KVH
    scale = HD ** (-0.5)
    offsets = jnp.arange(1, PATHS_PER_FOREST, dtype=jnp.int32)
    piece_locations = jnp.arange(TILE, dtype=jnp.int32)

    def one_tile(carry, tile_index):
        key_total, value_total = carry
        query_tile_row = lax.dynamic_index_in_dim(ancestors, tile_index, 0, keepdims=False)
        linked = jnp.sum(query_tile_row)
        nearest = jnp.min(jnp.where(query_tile_row > 0, offsets, PATHS_PER_FOREST))
        farthest = jnp.max(jnp.where(query_tile_row > 0, offsets, 0))
        sources = jnp.maximum(tile_index - jnp.stack([jnp.int32(0), nearest, farthest]), 0).astype(jnp.int32)
        present = [linked >= 0, linked >= 1, linked >= 2]
        start = (tile_index * TILE).astype(jnp.int32)
        query_block = lax.dynamic_slice_in_dim(queries, start, TILE, 0).astype(jnp.float32).reshape(TILE, KVH, group, HD)
        key_list = []
        value_list = []
        mask_list = []
        for slot in range(3):
            anchor = (sources[slot] * TILE).astype(jnp.int32)
            key_list.append(lax.dynamic_slice_in_dim(keys, anchor, TILE, 0))
            value_list.append(lax.dynamic_slice_in_dim(values, anchor, TILE, 0))
            valid = (piece_locations[None, :] < lengths[sources[slot]]) & present[slot]
            if slot == 0:
                valid = valid & (piece_locations[None, :] <= piece_locations[:, None])
            else:
                valid = jnp.broadcast_to(valid, (TILE, TILE))
            mask_list.append(valid)
        key_block = jnp.concatenate(key_list, 0).astype(jnp.float32).reshape(3 * TILE, KVH, HD)
        value_block = jnp.concatenate(value_list, 0).astype(jnp.float32).reshape(3 * TILE, KVH, HD)
        seen = jnp.concatenate(mask_list, 1)
        scores = jnp.einsum('qkgd,jkd->kgqj', query_block, key_block) * scale
        held = jnp.where(seen[None, None], scores, -1e+30)
        largest_logit = lax.optimization_barrier(jnp.max(held, -1))
        raised = jnp.exp(held - largest_logit[..., None])
        weights = (raised / lax.optimization_barrier(jnp.sum(raised, -1))[..., None]).astype(jnp.bfloat16)
        weights = lax.optimization_barrier(weights).astype(jnp.float32)
        output = jnp.einsum('kgqj,jkd->qkgd', weights, value_block)
        query_valid = piece_locations < lengths[tile_index]
        output = jnp.where(query_valid[:, None, None, None], output, 0.0)
        incoming = lax.dynamic_slice_in_dim(d_out, start, TILE, 0).astype(jnp.float32)
        cotangent = (advantage[tile_index] * incoming * query_valid[:, None].astype(jnp.float32)).astype(jnp.bfloat16)
        cotangent = lax.optimization_barrier(cotangent).astype(jnp.float32).reshape(TILE, KVH, group, HD)
        delta = jnp.einsum('qkgd,qkgd->kgq', cotangent, output)
        value_part = jnp.einsum('kgqj,qkgd->jkd', weights, cotangent)
        product = jnp.einsum('qkgd,jkd->kgqj', cotangent, value_block)
        slopes = (weights * (product - delta[..., None]) * scale).astype(jnp.bfloat16)
        slopes = lax.optimization_barrier(slopes).astype(jnp.float32)
        query_grad = jnp.einsum('kgqj,jkd->qkgd', slopes, key_block)
        key_part = jnp.einsum('kgqj,qkgd->jkd', slopes, query_block)
        key_part = key_part.reshape(3, TILE, KVH * HD)
        value_part = value_part.reshape(3, TILE, KVH * HD)
        for slot in range(3):
            anchor = (sources[slot] * TILE).astype(jnp.int32)
            current = lax.dynamic_slice_in_dim(key_total, anchor, TILE, 0)
            key_total = lax.dynamic_update_slice_in_dim(key_total, current + jnp.where(present[slot], key_part[slot], 0.0), anchor, 0)
            current = lax.dynamic_slice_in_dim(value_total, anchor, TILE, 0)
            value_total = lax.dynamic_update_slice_in_dim(value_total, current + jnp.where(present[slot], value_part[slot], 0.0), anchor, 0)
        tile_out = output.reshape(TILE, H * HD).astype(jnp.bfloat16)
        tile_grad = query_grad.reshape(TILE, H * HD).astype(jnp.bfloat16)
        return ((key_total, value_total), (tile_out, tile_grad))
    zeros_kv = jnp.zeros((TOKENS, KVH * HD), jnp.float32)
    (key_total, value_total), (tiles_out, tiles_grad) = lax.scan(one_tile, (zeros_kv, zeros_kv), jnp.arange(SEGS, dtype=jnp.int32))
    attended = tiles_out.reshape(TOKENS, H * HD)
    grad_queries = tiles_grad.reshape(TOKENS, H * HD)
    return (attended, grad_queries, key_total.astype(jnp.bfloat16), value_total.astype(jnp.bfloat16), advantage)
```

```python
import jax
import jax.numpy as jnp
from jax import lax
from jax.experimental import pallas as pl
from jax.experimental.pallas import tpu as pltpu
from jax.sharding import PartitionSpec as P

H = 32
KVH = 4
HD = 128
TILE = 256
HALF = 128
TREE = 8
GROUPS = 8
WIDE = 256
MESH = pl.DeviceIdType.MESH
SCALE = HD**-0.5
LOG2 = SCALE * 1.4426950408889634
NEG = -1e30
f32 = jnp.float32
bf16 = jnp.bfloat16
NT = (((1,), (1,)), ((), ()))
PARTS = ((0, 48), (48, 48), (96, 32))


def cols(index, size):
    return pl.ds(pl.multiple_of(index * size, size), size)


def dot(a, b):
    return jnp.dot(a, b, preferred_element_type=f32)


def dot_nt(a, b):
    return lax.dot_general(a, b, NT, preferred_element_type=f32)


def kernel(
    q_hbm, k_hbm, v_hbm, do_hbm, len_ref, anc_ref, rew_ref, pru_ref, grp_ref,
    att_hbm, dq_hbm, gk_ref, gv_ref, adv_ref,
    q_ref, do_ref, att_ref, dq_ref, kv, qT, doT, e_ref, oT, dqT, st, bias,
    near, far, total, mine, theirs, inbox, outbox,
    loc_sem, ag_send, ag_recv, core_send, core_recv, st_send, st_recv, rs_send, rs_recv,
):
    ctx = lax.axis_index("ctx")
    tp = lax.axis_index("tp")
    tree = ctx // TREE
    seg = ctx % TREE
    core = ctx % 2
    z = ((ctx // 2) % 2) * 2 + tp
    y = (ctx // 4) % 2
    first = tree * TREE

    def place(yy, zz, cc):
        zz = zz % 4
        return first + yy * 4 + (zz // 2) * 2 + cc, zz % 2

    def segment(yy, zz):
        zz = zz % 4
        return yy * 4 + (zz // 2) * 2 + core

    dev_core = place(y, z, 1 - core)
    dev_up = place(y, z + 1, core)
    dev_down = place(y, z + 3, core)
    dev_y = place(1 - y, z, core)
    links = (dev_up, dev_down, dev_y)
    kin = [(first + (seg + i) % TREE, tp) for i in range(1, TREE)]
    others = [(((tree + i) % 8) * TREE + seg, tp) for i in range(1, 8)]

    barrier = pltpu.get_barrier_semaphore()
    for device in kin + [dev_up, dev_down] + others:
        pl.semaphore_signal(barrier, inc=1, device_id=device, device_id_type=MESH)

    own_rows = pl.ds(tp * HALF, HALF)
    loads = [
        pltpu.make_async_copy(k_hbm, kv.at[seg, 0, own_rows], loc_sem.at[0]),
        pltpu.make_async_copy(v_hbm, kv.at[seg, 1, own_rows], loc_sem.at[1]),
        pltpu.make_async_copy(q_hbm, q_ref, loc_sem.at[2]),
        pltpu.make_async_copy(do_hbm, do_ref, loc_sem.at[3]),
    ]
    for load in loads:
        load.start()

    lane = lax.broadcasted_iota(jnp.int32, (8, 128), 1)
    row = lax.broadcasted_iota(jnp.int32, (8, 128), 0)
    reward = rew_ref[0]
    living = 1.0 - pru_ref[0].astype(f32)
    belongs = lane == grp_ref[0]
    parent = jnp.int32(0)
    for o in range(1, TREE):
        parent = parent + jnp.where(o < seg, anc_ref[0, o - 1] * (seg - o), 0)
    has_parent = parent > 0
    terms = jnp.where(row == 0, living, jnp.where(row == 1, living * reward, living * reward * reward))
    near[0] = jnp.where(
        row < 3, jnp.where(belongs, terms, 0.0), jnp.where(has_parent, parent, -1).astype(f32)
    )

    pl.semaphore_wait(barrier, 16)
    loads[0].wait()
    loads[1].wait()

    def block(yy, zz, start=0, size=HALF):
        zz = zz % 4
        return kv.at[segment(yy, zz), :, pl.ds(pl.multiple_of((zz % 2) * HALF + start, 16), size)]

    def send(ref, i, device, sends=ag_send, recvs=ag_recv):
        copy = pltpu.make_async_remote_copy(
            src_ref=ref, dst_ref=ref, send_sem=sends.at[i], recv_sem=recvs.at[i],
            device_id=device, device_id_type=MESH,
        )
        copy.start()
        return copy

    def forward(ref, i):
        return send(ref, i, dev_core, core_send, core_recv)

    ag = [send(block(y, z), i, links[i]) for i in range(3)]
    cores = [forward(block(y, z), 0)]
    notes = []
    for i in range(1, TREE):
        copy = pltpu.make_async_remote_copy(
            src_ref=near.at[0], dst_ref=near.at[i], send_sem=st_send.at[i], recv_sem=st_recv.at[i],
            device_id=kin[i - 1], device_id_type=MESH,
        )
        copy.start()
        notes.append(copy)

    own_len = len_ref[ctx]
    par_len = jnp.where(has_parent, len_ref[first + parent], 0)
    u = lax.broadcasted_iota(jnp.int32, (TILE, HALF), 0)
    t = lax.broadcasted_iota(jnp.int32, (TILE, HALF), 1) + tp * HALF
    bias[0] = jnp.where((u <= t) & (u < own_len), 0.0, NEG)
    bias[1] = jnp.where(u < par_len, 0.0, NEG)
    root_off = jnp.where(seg > 0, 0.0, -NEG)
    loads[2].wait()
    loads[3].wait()

    def turn(h, carry):
        qT[:, cols(h, HD)] = q_ref[:, cols(h, HD)].T
        doT[:, cols(h, HD)] = do_ref[:, cols(h, HD)].T
        return carry

    lax.fori_loop(0, H, turn, 0, unroll=4)

    for copy in notes:
        copy.wait_recv()
    summed = near[0]
    for i in range(1, TREE):
        summed = summed + near[i]
    far[0] = summed
    mate = jnp.where(core == 0, near[7], near[1])[3:4, 0:1]
    more = []
    for i in range(1, 8):
        copy = pltpu.make_async_remote_copy(
            src_ref=far.at[0], dst_ref=far.at[i], send_sem=st_send.at[7 + i],
            recv_sem=st_recv.at[7 + i], device_id=others[i - 1], device_id_type=MESH,
        )
        copy.start()
        more.append(copy)

    for copy in ag:
        copy.wait_recv()
    second = [
        send(block(1 - y, z), 3, dev_up),
        send(block(y, z + 1), 4, dev_down),
        send(block(y, z + 1), 5, dev_y),
    ]
    cores += [
        forward(block(y, z + 3), 1),
        forward(block(y, z + 1), 2),
        forward(block(1 - y, z), 3),
    ]

    def forward_own(k, carry):
        ko = kv[seg, 0, :, cols(k, HD)]
        vT = kv[seg, 1, :, cols(k, HD)].T
        b = jnp.concatenate([bias[0], bias[0]], 1)
        for p in range(4):
            c = cols(k * 4 + p, WIDE)
            s = dot(ko, qT[:, c]) + b
            m = jnp.max(s, 0, keepdims=True) * LOG2
            e = jnp.exp2(s * LOG2 - m)
            st[0:1, c] = m
            st[1:2, c] = jnp.sum(e, 0, keepdims=True)
            e = e.astype(bf16)
            e_ref[0:TILE, c] = e
            oT[:, c] = dot(vT, e)
        return carry

    lax.fori_loop(0, KVH, forward_own, 0)

    for copy in second:
        copy.wait_recv()
    (a0, an), (b0, bn), (c0, cn) = PARTS
    third = [
        send(block(1 - y, z + 3, b0, bn), 6, dev_up),
        send(block(1 - y, z + 1, a0, an), 7, dev_down),
        send(block(y, z + 2, c0, cn), 8, dev_y),
    ]
    cores += [
        forward(block(1 - y, z + 3), 4),
        forward(block(y, z + 2), 5),
        forward(block(1 - y, z + 1), 6),
    ]
    for copy in more:
        copy.wait_recv()
    summed = far[0]
    for i in range(1, 8):
        summed = summed + far[i]
    members = jnp.maximum(summed[0:1], 1.0)
    average = summed[1:2] / members
    spread = jnp.sqrt(jnp.maximum(summed[2:3] / members - average * average, 0.0))
    here = belongs[0:1]
    adv = (
        living
        * (reward - jnp.sum(jnp.where(here, average, 0.0), 1, keepdims=True))
        / jnp.sum(jnp.where(here, jnp.maximum(spread, 1.0), 0.0), 1, keepdims=True)
    )
    adv_ref[...] = jnp.broadcast_to(adv, (1, 128))
    for copy in third:
        copy.wait_recv()
    cores += [
        forward(block(1 - y, z + 2, b0, bn), 7),
        forward(block(1 - y, z + 2, a0, an), 8),
        forward(block(1 - y, z + 2, c0, cn), 9),
    ]
    for copy in cores:
        copy.wait_recv()
    for copy in ag + second + third + cores + notes + more:
        copy.wait_send()

    def forward_rest(k, carry):
        kr = kv[0, 0, :, cols(k, HD)]
        kp = kv[parent, 0, :, cols(k, HD)]
        vT = jnp.concatenate([kv[0, 1, :, cols(k, HD)], kv[parent, 1, :, cols(k, HD)]], 0).T
        b = jnp.concatenate([bias[1], bias[1]], 1)
        slot = lax.broadcasted_iota(jnp.int32, (1, WIDE), 1) % HALF + tp * HALF
        for p in range(4):
            c = cols(k * 4 + p, WIDE)
            sr = dot(kr, qT[:, c])
            sp = dot(kp, qT[:, c]) + b
            m2 = (
                jnp.maximum(jnp.max(sr, 0, keepdims=True) - root_off, jnp.max(sp, 0, keepdims=True))
                * LOG2
            )
            er = jnp.exp2(sr * LOG2 - (m2 + root_off))
            ep = jnp.exp2(sp * LOG2 - m2)
            l2 = jnp.sum(er, 0, keepdims=True) + jnp.sum(ep, 0, keepdims=True)
            e = jnp.concatenate([er, ep], 0).astype(bf16)
            e_ref[TILE : 3 * TILE, c] = e
            o2 = dot(vT, e)
            m1 = st[0:1, c]
            m = jnp.maximum(m1, m2)
            a1 = jnp.exp2(m1 - m)
            a2 = jnp.exp2(m2 - m)
            inv = jnp.where(slot < own_len, 1.0 / (st[1:2, c] * a1 + l2 * a2), 0.0)
            s1 = a1 * inv
            s2 = a2 * inv
            o = oT[:, c] * s1 + o2 * s2
            st[2:3, c] = s1
            st[3:4, c] = s2
            st[4:5, c] = jnp.sum(o * doT[:, c].astype(f32), 0, keepdims=True)
            o = o.T
            for i in range(2):
                att_ref[:, cols((k * 4 + p) * 2 + i, HD)] = o[i * HD : (i + 1) * HD].astype(bf16)
        return carry

    lax.fori_loop(0, KVH, forward_rest, 0)
    store_att = pltpu.make_async_copy(att_ref, att_hbm, loc_sem.at[0])
    store_att.start()

    def back(k, key, value, r0, n, scale_row, last):
        keyT = key.T
        dk = jnp.zeros((n, HD), f32)
        dv = jnp.zeros((n, HD), f32)
        for p in range(4):
            c = cols(k * 4 + p, WIDE)
            d = doT[:, c]
            e = e_ref[r0 : r0 + n, c]
            ds = (e.astype(f32) * (dot(value, d) - st[4:5, c])).astype(bf16)
            sr = st[scale_row : scale_row + 1, c]
            dk += dot_nt(ds, (qT[:, c].astype(f32) * sr).astype(bf16))
            dv += dot_nt(e, (d.astype(f32) * sr).astype(bf16))
            g = dot(keyT, ds) * (sr * (adv * SCALE))
            if last:
                g = (g + dqT[:, c]).T
                for i in range(2):
                    dq_ref[:, cols((k * 4 + p) * 2 + i, HD)] = g[i * HD : (i + 1) * HD].astype(bf16)
            else:
                dqT[:, c] = g
        return (dk * (adv * SCALE)).astype(bf16), (dv * adv).astype(bf16)

    def back_rest(k, carry):
        key = jnp.concatenate([kv[0, 0, :, cols(k, HD)], kv[parent, 0, :, cols(k, HD)]], 0)
        value = jnp.concatenate([kv[0, 1, :, cols(k, HD)], kv[parent, 1, :, cols(k, HD)]], 0)
        dk, dv = back(k, key, value, TILE, 2 * TILE, 3, False)
        for i in range(2):
            mine[i, 0, :, cols(k, HD)] = dk[i * TILE : (i + 1) * TILE]
            mine[i, 1, :, cols(k, HD)] = dv[i * TILE : (i + 1) * TILE]
        return carry

    lax.fori_loop(0, KVH, back_rest, 0)

    swap = pltpu.make_async_remote_copy(
        src_ref=mine.at[pl.ds(0, 2)], dst_ref=theirs, send_sem=core_send.at[10],
        recv_sem=core_recv.at[10], device_id=dev_core, device_id_type=MESH,
    )
    swap.start()
    swap.wait_recv()

    parent_mark = jnp.where(has_parent, parent, -1)

    def part(yy, zz, start=0, size=HALF):
        place_ = segment(yy, zz)
        rows = pl.ds(pl.multiple_of(((zz % 4) % 2) * HALF + start, 16), size)
        place_f = place_.astype(f32)
        own_w = jnp.where(parent_mark == place_, 1.0, 0.0)
        mate_w = jnp.where(mate == place_f, 1.0, 0.0)
        root_w = jnp.where(place_ == 0, 1.0, 0.0)
        return (
            mine[1, :, rows].astype(f32) * own_w
            + theirs[1, :, rows].astype(f32) * mate_w[None]
            + (mine[0, :, rows].astype(f32) + theirs[0, :, rows].astype(f32)) * root_w
        )

    def ship(i, value, device, start=0, size=HALF):
        rows = pl.ds(start, size)
        outbox[i, :, rows] = value.astype(bf16)
        copy = pltpu.make_async_remote_copy(
            src_ref=outbox.at[i, :, rows], dst_ref=inbox.at[i, :, rows], send_sem=rs_send.at[i],
            recv_sem=rs_recv.at[i], device_id=device, device_id_type=MESH,
        )
        copy.start()
        return copy

    zero_step = [
        ship(0, part(1 - y, z + 2, a0, an), dev_up, a0, an),
        ship(1, part(1 - y, z + 2, b0, bn), dev_down, b0, bn),
        ship(2, part(1 - y, z + 2, c0, cn), dev_y, c0, cn),
    ]

    def back_own(k, carry):
        dk, dv = back(k, kv[seg, 0, :, cols(k, HD)], kv[seg, 1, :, cols(k, HD)], 0, TILE, 2, True)
        mine[2, 0, :, cols(k, HD)] = dk
        mine[2, 1, :, cols(k, HD)] = dv
        return carry

    lax.fori_loop(0, 2, back_own, 0)

    def got(i, start=0, size=HALF):
        return inbox[i, :, pl.ds(start, size)].astype(f32)

    for copy in zero_step:
        copy.wait_recv()

    def padded(yy, zz, i, start, size):
        pieces = []
        if start > 0:
            pieces.append(part(yy, zz, 0, start))
        pieces.append(part(yy, zz, start, size) + got(i, start, size))
        if start + size < HALF:
            pieces.append(part(yy, zz, start + size, HALF - start - size))
        return jnp.concatenate(pieces, 1)

    one_step = [
        ship(3, padded(y, z + 2, 2, c0, cn), dev_up),
        ship(4, padded(1 - y, z + 3, 1, b0, bn), dev_down),
        ship(5, padded(1 - y, z + 1, 0, a0, an), dev_y),
    ]
    lax.fori_loop(2, KVH, back_own, 0)
    store_dq = pltpu.make_async_copy(dq_ref, dq_hbm, loc_sem.at[1])
    store_dq.start()
    for copy in one_step:
        copy.wait_recv()

    def own_part(zz):
        zz = zz % 4
        w = jnp.where(zz // 2 == z // 2, 1.0, 0.0)
        return mine[2, :, pl.ds(pl.multiple_of((zz % 2) * HALF, HALF), HALF)].astype(f32) * w

    two_step = [
        ship(6, part(y, z + 1) + got(3) + got(5) + own_part(z + 1), dev_up),
        ship(7, part(y, z + 3) + own_part(z + 3), dev_down),
        ship(8, part(1 - y, z) + got(4), dev_y),
    ]
    final = part(y, z) + own_part(z)
    for copy in two_step:
        copy.wait_recv()
    final = final + got(6) + got(7) + got(8)
    gk_ref[...] = final[0].astype(bf16)
    gv_ref[...] = final[1].astype(bf16)
    swap.wait_send()
    for copy in zero_step + one_step + two_step:
        copy.wait_send()
    store_att.wait()
    store_dq.wait()


def body(queries, keys, values, d_out, lengths, ancestors, rewards, pruned, branch_group):
    hbm = pl.BlockSpec(memory_space=pl.ANY)
    smem = pl.BlockSpec(memory_space=pltpu.SMEM)
    vmem = pl.BlockSpec(memory_space=pltpu.VMEM)
    dma = pltpu.SemaphoreType.DMA
    att, dq, gk, gv, adv = pl.pallas_call(
        kernel,
        out_shape=(
            jax.ShapeDtypeStruct((HALF, H * HD), bf16),
            jax.ShapeDtypeStruct((HALF, H * HD), bf16),
            jax.ShapeDtypeStruct((HALF, KVH * HD), bf16),
            jax.ShapeDtypeStruct((HALF, KVH * HD), bf16),
            jax.ShapeDtypeStruct((1, 128), f32),
        ),
        in_specs=[hbm] * 4 + [smem] * 5,
        out_specs=(hbm, hbm, vmem, vmem, vmem),
        scratch_shapes=[
            pltpu.VMEM((HALF, H * HD), bf16),
            pltpu.VMEM((HALF, H * HD), bf16),
            pltpu.VMEM((HALF, H * HD), bf16),
            pltpu.VMEM((HALF, H * HD), bf16),
            pltpu.VMEM((TREE, 2, TILE, KVH * HD), bf16),
            pltpu.VMEM((HD, H * HALF), bf16),
            pltpu.VMEM((HD, H * HALF), bf16),
            pltpu.VMEM((3 * TILE, H * HALF), bf16),
            pltpu.VMEM((HD, H * HALF), f32),
            pltpu.VMEM((HD, H * HALF), f32),
            pltpu.VMEM((8, H * HALF), f32),
            pltpu.VMEM((2, TILE, HALF), f32),
            pltpu.VMEM((8, 8, 128), f32),
            pltpu.VMEM((8, 8, 128), f32),
            pltpu.VMEM((8, 128), f32),
            pltpu.VMEM((3, 2, TILE, KVH * HD), bf16),
            pltpu.VMEM((2, 2, TILE, KVH * HD), bf16),
            pltpu.VMEM((9, 2, HALF, KVH * HD), bf16),
            pltpu.VMEM((9, 2, HALF, KVH * HD), bf16),
            dma((4,)),
            dma((9,)),
            dma((9,)),
            dma((11,)),
            dma((11,)),
            dma((15,)),
            dma((15,)),
            dma((9,)),
            dma((9,)),
        ],
        compiler_params=pltpu.CompilerParams(
            collective_id=0, has_side_effects=True, vmem_limit_bytes=56 << 20
        ),
        name="tree_attention",
    )(queries, keys, values, d_out, lengths, ancestors, rewards, pruned, branch_group)
    return att, dq, gk, gv, adv[0, :1]


def solution(mesh):
    rows = P(("ctx", "tp"), None)
    in_specs = (rows, rows, rows, rows, P(), P("ctx", None), P("ctx"), P("ctx"), P("ctx"))
    out_specs = (rows, rows, rows, rows, P("ctx"))
    return jax.shard_map(body, mesh=mesh, in_specs=in_specs, out_specs=out_specs, check_vma=False)
```

```python
import jax
import jax.numpy as jnp
from jax import lax
from jax.experimental import pallas as pl
from jax.experimental.pallas import tpu as pltpu
from jax.sharding import PartitionSpec as P

H = 32
KVH = 4
HD = 128
TILE = 256
HALF = 128
TREE = 8
GROUPS = 8
WIDE = 1024
MESH = pl.DeviceIdType.MESH
SCALE = HD**-0.5
LOG2 = SCALE * 1.4426950408889634
NEG = -1e30
f32 = jnp.float32
bf16 = jnp.bfloat16
NT = (((1,), (1,)), ((), ()))
SPLIT = 80


def cols(index, size):
    return pl.ds(pl.multiple_of(index * size, size), size)


def dot(a, b):
    return jnp.dot(a, b, preferred_element_type=f32)


def dot_nt(a, b):
    return lax.dot_general(a, b, NT, preferred_element_type=f32)


def kernel(
    q_hbm, k_hbm, v_hbm, do_hbm, len_hbm, anc_hbm, rew_hbm, pru_hbm, grp_hbm,
    att_hbm, dq_hbm, gk_hbm, gv_hbm, adv_hbm,
    q_ref, do_ref, att_ref, dq_ref, gk_ref, gv_ref, adv_ref,
    len_ref, anc_ref, rew_ref, pru_ref, grp_ref,
    kv, qT, doT, bias, near, far, mine, theirs, inbox, outbox,
    loc_sem, out_sem, ag_send, ag_recv, core_send, core_recv, st_send, st_recv, rs_send, rs_recv,
):
    ctx = lax.axis_index("ctx")
    tp = lax.axis_index("tp")
    tree = ctx // TREE
    seg = ctx % TREE
    core = ctx % 2
    z = ((ctx // 2) % 2) * 2 + tp
    y = (ctx // 4) % 2
    first = tree * TREE

    def place(yy, zz, cc):
        zz = zz % 4
        return first + yy * 4 + (zz // 2) * 2 + cc, zz % 2

    dev_core = place(y, z, 1 - core)
    dev_up = place(y, z + 1, core)
    dev_down = place(y, z + 3, core)
    dev_far = place(y, z + 2, core)
    dev_y = place(1 - y, z, core)
    kin = [(first + (seg + i) % TREE, tp) for i in range(1, TREE)]
    others = [(((tree + i) % 8) * TREE + seg, tp) for i in range(1, 8)]

    barrier = pltpu.get_barrier_semaphore()
    for device in kin + [dev_up, dev_down] + others:
        pl.semaphore_signal(barrier, inc=1, device_id=device, device_id_type=MESH)

    small = [
        pltpu.make_async_copy(a, b, loc_sem.at[i])
        for i, (a, b) in enumerate(
            zip(
                (len_hbm, anc_hbm, rew_hbm, pru_hbm, grp_hbm),
                (len_ref, anc_ref, rew_ref, pru_ref, grp_ref),
            )
        )
    ]
    rows_here = pl.ds(tp * HALF, HALF)
    large = [
        pltpu.make_async_copy(q_hbm, q_ref, loc_sem.at[5]),
        pltpu.make_async_copy(do_hbm, do_ref, loc_sem.at[6]),
    ]
    own_kv = []
    for h in range(KVH):
        for i, ref in enumerate((k_hbm, v_hbm)):
            own_kv.append(
                pltpu.make_async_copy(
                    ref.at[:, pl.ds(h * HD, HD)],
                    kv.at[h, core, y * 2 + z // 2, i, rows_here],
                    loc_sem.at[7 + 2 * h + i],
                )
            )
    for copy in small + large + own_kv:
        copy.start()
    for copy in small:
        copy.wait()

    lane = lax.broadcasted_iota(jnp.int32, (8, 128), 1)
    row = lax.broadcasted_iota(jnp.int32, (8, 128), 0)
    reward = rew_ref[0]
    living = 1.0 - pru_ref[0].astype(f32)
    belongs = lane == grp_ref[0]
    parent = jnp.int32(0)
    for o in range(1, TREE):
        parent = parent + jnp.where(o < seg, anc_ref[0, o - 1] * (seg - o), 0)
    has_parent = parent > 0
    terms = jnp.where(
        row == 0, living, jnp.where(row == 1, living * reward, living * reward * reward)
    )
    near[0] = jnp.where(
        row < 3, jnp.where(belongs, terms, 0.0), jnp.where(has_parent, parent, -1).astype(f32)
    )

    own_len = len_ref[ctx]
    par_len = jnp.where(has_parent, len_ref[first + parent], 0)
    u = lax.broadcasted_iota(jnp.int32, (TILE, HALF), 0)
    t = lax.broadcasted_iota(jnp.int32, (TILE, HALF), 1) + tp * HALF
    bias[0] = jnp.where((u <= t) & (u < own_len), 0.0, NEG)
    bias[1] = jnp.where(u < par_len, 0.0, NEG)
    root_off = jnp.where(seg > 0, 0.0, -NEG)
    slot = lax.broadcasted_iota(jnp.int32, (1, WIDE), 1) % HALF + tp * HALF
    seen = slot < own_len
    for copy in large:
        copy.wait()

    def turn(h, carry):
        qT[:, cols(h, HD)] = q_ref[:, cols(h, HD)].T
        doT[:, cols(h, HD)] = do_ref[:, cols(h, HD)].T
        return carry

    lax.fori_loop(0, H, turn, 0, unroll=4)
    for copy in own_kv:
        copy.wait()
    pl.semaphore_wait(barrier, 16)

    def remote(src, dst, device, sends, recvs, i):
        return pltpu.make_async_remote_copy(
            src_ref=src, dst_ref=dst, send_sem=sends.at[i], recv_sem=recvs.at[i],
            device_id=device, device_id_type=MESH,
        )

    def start(copies):
        for copy in copies:
            copy.start()

    def receive(copies):
        for copy in copies:
            copy.wait_recv()

    def block(h, yy, zz, begin=0, size=HALF):
        zz = zz % 4
        return kv.at[
            h, core, yy * 2 + zz // 2, :, pl.ds(pl.multiple_of((zz % 2) * HALF + begin, 16), size)
        ]

    def gather(h, pieces, base):
        return [
            remote(ref, ref, device, ag_send, ag_recv, h * 9 + base + i)
            for i, (ref, device) in enumerate(pieces)
        ]

    def gather_one(h):
        here = block(h, y, z)
        return gather(h, [(here, dev_up), (here, dev_down), (here, dev_y), (here, dev_far)], 0)

    def gather_two(h):
        over = block(h, 1 - y, z, 0, SPLIT)
        rest = HALF - SPLIT
        return gather(
            h,
            [
                (over, dev_up),
                (over, dev_down),
                (block(h, y, z + 1, SPLIT, rest), dev_y),
                (block(h, y, z + 3, SPLIT, rest), dev_y),
                (block(h, y, z + 2), dev_y),
            ],
            4,
        )

    def share(h, yy, i):
        ref = kv.at[h, core, pl.ds(yy * 2, 2)]
        return [remote(ref, ref, dev_core, core_send, core_recv, h * 3 + i)]

    def share_one(h):
        return share(h, y, 0)

    def share_two(h):
        return share(h, 1 - y, 1)

    notes = [
        remote(near.at[0], near.at[i], kin[i - 1], st_send, st_recv, i) for i in range(1, TREE)
    ]
    more = [
        remote(far.at[0], far.at[i], others[i - 1], st_send, st_recv, 7 + i) for i in range(1, 8)
    ]

    start(gather_one(0))
    start(notes)
    start(gather_one(1))
    receive(gather_one(0))
    start(gather_two(0) + share_one(0) + gather_one(2))
    receive(notes)
    summed = near[0]
    for i in range(1, TREE):
        summed = summed + near[i]
    far[0] = summed
    mate = jnp.where(core == 0, near[7], near[1])[3:4, 0:1]
    start(more)
    receive(gather_one(1))
    start(gather_two(1) + share_one(1) + gather_one(3))
    receive(gather_two(0))
    start(share_two(0))
    receive(more)
    summed = far[0]
    for i in range(1, 8):
        summed = summed + far[i]
    members = jnp.maximum(summed[0:1], 1.0)
    average = summed[1:2] / members
    spread = jnp.sqrt(jnp.maximum(summed[2:3] / members - average * average, 0.0))
    here = belongs[0:1]
    adv = (
        living
        * (reward - jnp.sum(jnp.where(here, average, 0.0), 1, keepdims=True))
        / jnp.sum(jnp.where(here, jnp.maximum(spread, 1.0), 0.0), 1, keepdims=True)
    )
    adv_ref[...] = jnp.broadcast_to(adv, (8, 128))
    store_adv = pltpu.make_async_copy(adv_ref, adv_hbm, out_sem.at[0])
    store_adv.start()

    def swap(h):
        return [
            remote(
                mine.at[h, pl.ds(0, 2)], theirs.at[h], dev_core, core_send, core_recv, h * 3 + 2
            )
        ]

    parent_mark = jnp.where(has_parent, parent, -1)

    def part(h, yy, zz, begin=0, size=HALF):
        zz = zz % 4
        target = yy * 4 + (zz // 2) * 2 + core
        rows = pl.ds(pl.multiple_of((zz % 2) * HALF + begin, 16), size)
        own_w = jnp.where(parent_mark == target, 1.0, 0.0)
        mate_w = jnp.where(mate == target.astype(f32), 1.0, 0.0)
        root_w = jnp.where(target == 0, 1.0, 0.0)
        return (
            mine[h, 1, :, rows].astype(f32) * own_w
            + theirs[h, 1, :, rows].astype(f32) * mate_w[None]
            + (mine[h, 0, :, rows].astype(f32) + theirs[h, 0, :, rows].astype(f32)) * root_w
        )

    def own_part(h, zz):
        zz = zz % 4
        w = jnp.where(zz // 2 == z // 2, 1.0, 0.0)
        rows = pl.ds(pl.multiple_of((zz % 2) * HALF, HALF), HALF)
        return mine[h, 2, :, rows].astype(f32) * w

    low = pl.ds(0, SPLIT)
    high = pl.ds(SPLIT, HALF - SPLIT)
    whole = pl.ds(0, HALF)

    def ship(h, i, rows, device):
        return remote(
            outbox.at[h, i, :, rows], inbox.at[h, i, :, rows], device, rs_send, rs_recv, h * 9 + i
        )

    def reduce_one(h):
        return [
            ship(h, 0, low, dev_up),
            ship(h, 1, low, dev_down),
            ship(h, 2, high, dev_y),
            ship(h, 3, high, dev_y),
            ship(h, 4, whole, dev_y),
        ]

    def reduce_two(h):
        return [
            ship(h, 5, whole, dev_y),
            ship(h, 6, whole, dev_up),
            ship(h, 7, whole, dev_down),
            ship(h, 8, whole, dev_far),
        ]

    def fill_one(h):
        up = part(h, 1 - y, z + 1).astype(bf16)
        down = part(h, 1 - y, z + 3).astype(bf16)
        outbox[h, 0, :, low] = up[:, :SPLIT]
        outbox[h, 1, :, low] = down[:, :SPLIT]
        outbox[h, 2, :, high] = up[:, SPLIT:]
        outbox[h, 3, :, high] = down[:, SPLIT:]
        outbox[h, 4] = part(h, 1 - y, z + 2).astype(bf16)

    def got(h, i, rows=whole):
        return inbox[h, i, :, rows].astype(f32)

    def fill_two(h):
        over = part(h, 1 - y, z)
        outbox[h, 5, :, low] = (over[:, :SPLIT] + got(h, 0, low) + got(h, 1, low)).astype(bf16)
        outbox[h, 5, :, high] = over[:, SPLIT:].astype(bf16)
        for i, zz in ((6, z + 1), (7, z + 3)):
            side = part(h, y, zz) + own_part(h, zz)
            outbox[h, i, :, low] = side[:, :SPLIT].astype(bf16)
            outbox[h, i, :, high] = (side[:, SPLIT:] + got(h, i - 4, high)).astype(bf16)
        outbox[h, 8] = (part(h, y, z + 2) + got(h, 4)).astype(bf16)

    def close(h):
        total = part(h, y, z) + own_part(h, z)
        for i in range(5, 9):
            total = total + got(h, i)
        gk_ref[:, cols(h, HD)] = total[0].astype(bf16)
        gv_ref[:, cols(h, HD)] = total[1].astype(bf16)

    def store(h, i):
        ref, out = ((att_ref, att_hbm), (dq_ref, dq_hbm))[i]
        c = cols(h, WIDE)
        return pltpu.make_async_copy(ref.at[:, c], out.at[:, c], out_sem.at[1 + 2 * h + i])

    def head(h, carry):
        receive(share_one(h) + share_two(h))
        c = cols(h, WIDE)

        @pl.when(h == 3)
        def _():
            receive(reduce_one(0))
            fill_two(0)
            start(reduce_two(0))

        def tiles(i):
            chosen = kv[h, 1, 0, i]
            for other in range(2, TREE - 1):
                chosen = jnp.where(parent == other, kv[h, other % 2, other // 2, i], chosen)
            return jnp.concatenate(
                [kv[h, core, y * 2 + z // 2, i], kv[h, 0, 0, i], chosen], 0
            )

        key = tiles(0)
        value = tiles(1)
        s = dot(key, qT[:, c])
        so = s[:TILE] + jnp.concatenate([bias[0]] * 8, 1)
        sr = s[TILE : 2 * TILE]
        sp = s[2 * TILE :] + jnp.concatenate([bias[1]] * 8, 1)
        m = (
            jnp.maximum(
                jnp.maximum(jnp.max(so, 0, keepdims=True), jnp.max(sp, 0, keepdims=True)),
                jnp.max(sr, 0, keepdims=True) - root_off,
            )
            * LOG2
        )
        eo = jnp.exp2(so * LOG2 - m)
        er = jnp.exp2(sr * LOG2 - (m + root_off))
        ep = jnp.exp2(sp * LOG2 - m)
        inv = jnp.where(seen, 1.0 / jnp.sum(eo + er + ep, 0, keepdims=True), 0.0)
        e = jnp.concatenate([eo, er, ep], 0).astype(bf16)
        o = dot(value.T, e) * inv
        d = doT[:, c]
        delta = jnp.sum(o * d.astype(f32), 0, keepdims=True)
        o = o.T
        for i in range(8):
            att_ref[:, cols(h * 8 + i, HD)] = o[i * HD : (i + 1) * HD].astype(bf16)
        store(h, 0).start()

        @pl.when(h < 2)
        def _():
            receive(gather_one(h + 2))
            start(gather_two(h + 2) + share_one(h + 2))

        @pl.when(h < 3)
        def _():
            receive(gather_two(h + 1))
            start(share_two(h + 1))

        @pl.when(h > 0)
        def _():
            receive(swap(h - 1))
            fill_one(h - 1)
            start(reduce_one(h - 1))

        ds = (e.astype(f32) * (dot(value, d) - delta)).astype(bf16)
        dk = dot_nt(ds, (qT[:, c].astype(f32) * inv).astype(bf16)) * (adv * SCALE)
        dv = dot_nt(e, (d.astype(f32) * inv).astype(bf16)) * adv
        for i, place_ in enumerate((2, 0, 1)):
            mine[h, place_, 0] = dk[i * TILE : (i + 1) * TILE].astype(bf16)
            mine[h, place_, 1] = dv[i * TILE : (i + 1) * TILE].astype(bf16)
        start(swap(h))
        g = (dot(key.T, ds) * (inv * (adv * SCALE))).T
        for i in range(8):
            dq_ref[:, cols(h * 8 + i, HD)] = g[i * HD : (i + 1) * HD].astype(bf16)
        store(h, 1).start()
        return carry

    lax.fori_loop(0, KVH, head, 0)

    def second(h):
        receive(reduce_one(h))
        fill_two(h)
        start(reduce_two(h))

    second(1)
    receive(swap(3))
    fill_one(3)
    start(reduce_one(3))
    second(2)
    receive(reduce_two(0))
    close(0)
    second(3)
    for h in range(1, KVH):
        receive(reduce_two(h))
        close(h)
    stores = [
        pltpu.make_async_copy(gk_ref, gk_hbm, out_sem.at[9]),
        pltpu.make_async_copy(gv_ref, gv_hbm, out_sem.at[10]),
    ]
    start(stores)
    for copy in stores + [store_adv] + [store(h, i) for h in range(KVH) for i in range(2)]:
        copy.wait()
    for copy in notes + more:
        copy.wait_send()

    def drain(h, carry):
        sent = gather_one(h) + gather_two(h) + share_one(h) + share_two(h)
        for copy in sent + swap(h) + reduce_one(h) + reduce_two(h):
            copy.wait_send()
        return carry

    lax.fori_loop(0, KVH, drain, 0)


def finish(*refs):
    ins, outs, bufs, adv_out = refs[:5], refs[5:9], refs[10:15], refs[9]
    arrive, leave = refs[15], refs[16]
    loads = [pltpu.make_async_copy(ins[i], bufs[i], arrive.at[i]) for i in range(5)]
    stores = [pltpu.make_async_copy(bufs[i], outs[i], leave.at[i]) for i in range(4)]
    for copy in loads:
        copy.start()
    for load, copy in zip(loads, stores):
        load.wait()
        copy.start()
    loads[4].wait()
    adv_out[0] = bufs[4][0, 0]
    for copy in stores:
        copy.wait()


def body(queries, keys, values, d_out, lengths, ancestors, rewards, pruned, branch_group):
    hbm = pl.BlockSpec(memory_space=pl.ANY)
    dma = pltpu.SemaphoreType.DMA
    wide = jax.ShapeDtypeStruct((HALF, H * HD), bf16)
    narrow = jax.ShapeDtypeStruct((HALF, KVH * HD), bf16)
    i32 = jnp.int32
    results = pl.pallas_call(
        kernel,
        out_shape=(wide, wide, narrow, narrow, jax.ShapeDtypeStruct((8, 128), f32)),
        in_specs=[hbm] * 9,
        out_specs=(hbm,) * 5,
        scratch_shapes=[
            pltpu.VMEM((HALF, H * HD), bf16),
            pltpu.VMEM((HALF, H * HD), bf16),
            pltpu.VMEM((HALF, H * HD), bf16),
            pltpu.VMEM((HALF, H * HD), bf16),
            pltpu.VMEM((HALF, KVH * HD), bf16),
            pltpu.VMEM((HALF, KVH * HD), bf16),
            pltpu.VMEM((8, 128), f32),
            pltpu.SMEM(lengths.shape, i32),
            pltpu.SMEM(ancestors.shape, i32),
            pltpu.SMEM((1,), f32),
            pltpu.SMEM((1,), i32),
            pltpu.SMEM((1,), i32),
            pltpu.VMEM((KVH, 2, 4, 2, TILE, HD), bf16),
            pltpu.VMEM((HD, H * HALF), bf16),
            pltpu.VMEM((HD, H * HALF), bf16),
            pltpu.VMEM((2, TILE, HALF), f32),
            pltpu.VMEM((8, 8, 128), f32),
            pltpu.VMEM((8, 8, 128), f32),
            pltpu.VMEM((KVH, 3, 2, TILE, HD), bf16),
            pltpu.VMEM((KVH, 2, 2, TILE, HD), bf16),
            pltpu.VMEM((KVH, 9, 2, HALF, HD), bf16),
            pltpu.VMEM((KVH, 9, 2, HALF, HD), bf16),
            dma((15,)),
            dma((11,)),
            dma((36,)),
            dma((36,)),
            dma((12,)),
            dma((12,)),
            dma((15,)),
            dma((15,)),
            dma((36,)),
            dma((36,)),
        ],
        compiler_params=pltpu.CompilerParams(
            collective_id=0, has_side_effects=True, vmem_limit_bytes=56 << 20
        ),
        name="tree_attention",
    )(queries, keys, values, d_out, lengths, ancestors, rewards, pruned, branch_group)
    return pl.pallas_call(
        finish,
        out_shape=(wide, wide, narrow, narrow, jax.ShapeDtypeStruct((1,), f32)),
        in_specs=[hbm] * 5,
        out_specs=(hbm,) * 4 + (pl.BlockSpec(memory_space=pltpu.SMEM),),
        scratch_shapes=[pltpu.VMEM(a.shape, a.dtype) for a in results] + [dma((5,)), dma((4,))],
        name="finish",
    )(*results)


def solution(mesh):
    rows = P(("ctx", "tp"), None)
    in_specs = (rows, rows, rows, rows, P(), P("ctx", None), P("ctx"), P("ctx"), P("ctx"))
    out_specs = (rows, rows, rows, rows, P("ctx"))
    return jax.shard_map(body, mesh=mesh, in_specs=in_specs, out_specs=out_specs, check_vma=False)
```

```python
import jax
import jax.numpy as jnp
from jax import lax
from jax.experimental import pallas as pl
from jax.experimental.pallas import tpu as pltpu
from jax.sharding import PartitionSpec as P

H = 32
KVH = 4
HD = 128
TILE = 256
HALF = 128
TREE = 8
GROUPS = 8
WIDE = 1024
MESH = pl.DeviceIdType.MESH
SCALE = HD**-0.5
LOG2 = SCALE * 1.4426950408889634
NEG = -1e30
f32 = jnp.float32
bf16 = jnp.bfloat16
NT = (((1,), (1,)), ((), ()))
SPLIT = 64


def cols(index, size):
    return pl.ds(pl.multiple_of(index * size, size), size)


def dot(a, b):
    return jnp.dot(a, b, preferred_element_type=f32)


def dot_nt(a, b):
    return lax.dot_general(a, b, NT, preferred_element_type=f32)


def kernel(
    q_hbm, k_hbm, v_hbm, do_hbm, len_hbm, anc_hbm, rew_hbm, pru_hbm, grp_hbm,
    att_hbm, dq_hbm, gk_hbm, gv_hbm, adv_hbm,
    q_ref, do_ref, att_ref, dq_ref, gk_ref, gv_ref, adv_ref,
    len_ref, anc_ref, rew_ref, pru_ref, grp_ref,
    kv, qT, doT, bias, near, far, mine, theirs, inbox, outbox,
    loc_sem, ag_send, ag_recv, core_send, core_recv, st_send, st_recv, rs_recv,
):
    ctx = lax.axis_index("ctx")
    tp = lax.axis_index("tp")
    tree = ctx // TREE
    seg = ctx % TREE
    core = ctx % 2
    z = ((ctx // 2) % 2) * 2 + tp
    y = (ctx // 4) % 2
    first = tree * TREE

    def place(yy, zz, cc):
        zz = zz % 4
        return first + yy * 4 + (zz // 2) * 2 + cc, zz % 2

    dev_core = place(y, z, 1 - core)
    pair = z + 1 - 2 * (z % 2)
    side = z + 3 + 2 * (z % 2)
    dev_pair = place(y, pair, core)
    dev_side = place(y, side, core)
    dev_far = place(y, z + 2, core)
    dev_y = place(1 - y, z, core)
    kin = [(first + (seg + i) % TREE, tp) for i in range(1, TREE)]
    others = [(((tree + i) % 8) * TREE + seg, tp) for i in range(1, 8)]

    barrier = pltpu.get_barrier_semaphore()
    for device in kin + [dev_pair, dev_side] + others:
        pl.semaphore_signal(barrier, inc=1, device_id=device, device_id_type=MESH)

    small = [
        pltpu.make_async_copy(a, b, loc_sem.at[i])
        for i, (a, b) in enumerate(
            zip(
                (len_hbm, anc_hbm, rew_hbm, pru_hbm, grp_hbm),
                (len_ref, anc_ref, rew_ref, pru_ref, grp_ref),
            )
        )
    ]
    rows_here = pl.ds(tp * HALF, HALF)
    large = [
        pltpu.make_async_copy(q_hbm, q_ref, loc_sem.at[5]),
        pltpu.make_async_copy(do_hbm, do_ref, loc_sem.at[6]),
    ]
    own_kv = []
    for h in range(KVH):
        for i, ref in enumerate((k_hbm, v_hbm)):
            own_kv.append(
                pltpu.make_async_copy(
                    ref.at[:, pl.ds(h * HD, HD)],
                    kv.at[h, core, y * 2 + z // 2, i, rows_here],
                    loc_sem.at[7 + 2 * h + i],
                )
            )
    for copy in small + large + own_kv:
        copy.start()
    for copy in small:
        copy.wait()

    lane = lax.broadcasted_iota(jnp.int32, (8, 128), 1)
    row = lax.broadcasted_iota(jnp.int32, (8, 128), 0)
    reward = rew_ref[0]
    living = 1.0 - pru_ref[0].astype(f32)
    belongs = lane == grp_ref[0]
    parent = jnp.int32(0)
    for o in range(1, TREE):
        parent = parent + jnp.where(o < seg, anc_ref[0, o - 1] * (seg - o), 0)
    has_parent = parent > 0
    terms = jnp.where(
        row == 0, living, jnp.where(row == 1, living * reward, living * reward * reward)
    )
    near[0] = jnp.where(
        row < 3, jnp.where(belongs, terms, 0.0), jnp.where(has_parent, parent, -1).astype(f32)
    )

    for copy in own_kv:
        copy.wait()
    pl.semaphore_wait(barrier, 16)

    def remote(src, dst, device, sends, recvs, i):
        return pltpu.make_async_remote_copy(
            src_ref=src, dst_ref=dst, send_sem=sends.at[i], recv_sem=recvs.at[i],
            device_id=device, device_id_type=MESH,
        )

    def act(method, moves, which):
        for move in moves:
            operation = getattr(move[0], method)
            if move[which] is None:
                operation()
            else:
                pl.when(move[which])(operation)

    def start(moves):
        act("start", moves, 1)

    def receive(moves):
        act("wait_recv", moves, 2)

    def sent(moves):
        act("wait_send", moves, 1)

    lower = y == 0
    upper = y == 1

    def block(h, yy, zz, begin=0, size=HALF):
        zz = zz % 4
        return kv.at[
            h, core, yy * 2 + zz // 2, :, pl.ds(pl.multiple_of((zz % 2) * HALF + begin, 16), size)
        ]

    def gather(h, pieces, base):
        return [
            (remote(ref, ref, device, ag_send, ag_recv, h * 8 + base + i), sends, gets)
            for i, (ref, device, sends, gets) in enumerate(pieces)
        ]

    def gather_one(h):
        here = block(h, y, z)
        return gather(
            h,
            [
                (here, dev_pair, None, None),
                (here, dev_side, lower | (z < 2), lower | (z >= 2)),
                (here, dev_y, lower, upper),
                (here, dev_far, lower | (z < 2), lower | (z >= 2)),
            ],
            0,
        )

    def gather_two(h):
        rest = HALF - SPLIT
        return gather(
            h,
            [
                (block(h, 1 - y, z), dev_pair, upper, upper),
                (block(h, 1 - y, z, 0, SPLIT), dev_side, upper, upper),
                (block(h, y, side, SPLIT, rest), dev_y, lower, upper),
                (block(h, y, z + 2), dev_y, lower, upper),
            ],
            4,
        )

    def share(h, yy, i, needed):
        ref = kv.at[h, core, pl.ds(yy * 2, 2)]
        return [(remote(ref, ref, dev_core, core_send, core_recv, h * 3 + i), needed, needed)]

    def share_one(h):
        return share(h, y, 0, None)

    def share_two(h):
        return share(h, 1 - y, 1, upper)

    notes = [
        (remote(near.at[0], near.at[i], kin[i - 1], st_send, st_recv, i), None, None)
        for i in range(1, TREE)
    ]
    more = [
        (
            pltpu.make_async_remote_copy(
                src_ref=far.at[0], dst_ref=far.at[i], send_sem=st_send.at[i],
                recv_sem=st_recv.at[7 + i], device_id=others[i - 1], device_id_type=MESH,
            ),
            None,
            None,
        )
        for i in range(1, 8)
    ]

    start(gather_one(0))
    start(notes)
    start(gather_one(1))

    own_len = len_ref[ctx]
    par_len = jnp.where(has_parent, len_ref[first + parent], 0)
    u = lax.broadcasted_iota(jnp.int32, (TILE, HALF), 0)
    t = lax.broadcasted_iota(jnp.int32, (TILE, HALF), 1) + tp * HALF
    bias[0] = jnp.where((u <= t) & (u < own_len), 0.0, NEG)
    bias[1] = jnp.where(u < par_len, 0.0, NEG)
    root_off = jnp.where(seg > 0, 0.0, -NEG)
    slot = lax.broadcasted_iota(jnp.int32, (1, WIDE), 1) % HALF + tp * HALF
    seen = slot < own_len
    for copy in large:
        copy.wait()

    def turn(h, carry):
        qT[:, cols(h, HD)] = q_ref[:, cols(h, HD)].T
        doT[:, cols(h, HD)] = do_ref[:, cols(h, HD)].T
        return carry

    lax.fori_loop(0, H, turn, 0, unroll=4)

    receive(gather_one(0))
    start(gather_two(0) + share_one(0) + gather_one(2))
    receive(notes)
    summed = near[0]
    for i in range(1, TREE):
        summed = summed + near[i]
    far[0] = summed
    mate = jnp.where(core == 0, near[7], near[1])[3:4, 0:1]
    sent(notes)
    start(more)
    receive(gather_one(1))
    start(gather_two(1) + share_one(1) + gather_one(3))
    receive(gather_two(0))
    start(share_two(0))
    receive(more)
    summed = far[0]
    for i in range(1, 8):
        summed = summed + far[i]
    members = jnp.maximum(summed[0:1], 1.0)
    average = summed[1:2] / members
    spread = jnp.sqrt(jnp.maximum(summed[2:3] / members - average * average, 0.0))
    here = belongs[0:1]
    adv = (
        living
        * (reward - jnp.sum(jnp.where(here, average, 0.0), 1, keepdims=True))
        / jnp.sum(jnp.where(here, jnp.maximum(spread, 1.0), 0.0), 1, keepdims=True)
    )
    adv_ref[...] = jnp.broadcast_to(adv, (8, 128))
    store_adv = pltpu.make_async_copy(adv_ref, adv_hbm, loc_sem.at[0])
    store_adv.start()

    def swap(h):
        copy = remote(
            mine.at[h, pl.ds(0, 2)], theirs.at[h], dev_core, core_send, core_recv, h * 3 + 2
        )
        return [(copy, None, None)]

    parent_mark = jnp.where(has_parent, parent, -1)

    def part(h, yy, zz, begin=0, size=HALF):
        zz = zz % 4
        target = yy * 4 + (zz // 2) * 2 + core
        rows = pl.ds(pl.multiple_of((zz % 2) * HALF + begin, 16), size)
        own_w = jnp.where(parent_mark == target, 1.0, 0.0)
        mate_w = jnp.where(mate == target.astype(f32), 1.0, 0.0)
        root_w = jnp.where(target == 0, 1.0, 0.0)
        return (
            mine[h, 1, :, rows].astype(f32) * own_w
            + theirs[h, 1, :, rows].astype(f32) * mate_w[None]
            + (mine[h, 0, :, rows].astype(f32) + theirs[h, 0, :, rows].astype(f32)) * root_w
        )

    def own_part(h, zz):
        rows = pl.ds(pl.multiple_of((zz % 2) * HALF, HALF), HALF)
        return mine[h, 2, :, rows].astype(f32)

    low = pl.ds(0, SPLIT)
    high = pl.ds(SPLIT, HALF - SPLIT)
    whole = pl.ds(0, HALF)

    def ship(h, i, rows, device, sends, gets):
        copy = remote(
            outbox.at[h, i, :, rows], inbox.at[h, i, :, rows], device, ag_send, rs_recv, h * 8 + i
        )
        return copy, sends, gets

    def reduce_one(h):
        return [
            ship(h, 0, whole, dev_pair, upper, upper),
            ship(h, 1, low, dev_side, upper, upper),
            ship(h, 2, high, dev_y, upper, lower),
            ship(h, 3, whole, dev_y, upper, lower),
        ]

    def reduce_two(h):
        return [
            ship(h, 4, whole, dev_y, upper, lower),
            ship(h, 5, whole, dev_pair, None, None),
            ship(h, 6, whole, dev_side, lower | (z >= 2), lower | (z < 2)),
            ship(h, 7, whole, dev_far, lower | (z >= 2), lower | (z < 2)),
        ]

    def fill_one(h):
        @pl.when(upper)
        def _():
            outbox[h, 0] = part(h, 1 - y, pair).astype(bf16)
            beside = part(h, 1 - y, side).astype(bf16)
            outbox[h, 1, :, low] = beside[:, :SPLIT]
            outbox[h, 2, :, high] = beside[:, SPLIT:]
            outbox[h, 3] = part(h, 1 - y, z + 2).astype(bf16)

    def got(h, i, rows=whole):
        return inbox[h, i, :, rows].astype(f32)

    def fill_two(h):
        outbox[h, 5] = (part(h, y, pair) + own_part(h, pair)).astype(bf16)

        @pl.when(upper)
        def _():
            over = part(h, 1 - y, z) + got(h, 0)
            outbox[h, 4, :, low] = (over[:, :SPLIT] + got(h, 1, low)).astype(bf16)
            outbox[h, 4, :, high] = over[:, SPLIT:].astype(bf16)
            outbox[h, 6] = part(h, y, side).astype(bf16)
            outbox[h, 7] = part(h, y, z + 2).astype(bf16)

        @pl.when(lower)
        def _():
            beside = part(h, y, side)
            outbox[h, 6, :, low] = beside[:, :SPLIT].astype(bf16)
            outbox[h, 6, :, high] = (beside[:, SPLIT:] + got(h, 2, high)).astype(bf16)
            outbox[h, 7] = (part(h, y, z + 2) + got(h, 3)).astype(bf16)

    def close(h):
        total = part(h, y, z) + own_part(h, z)
        for i, (_, _, gets) in enumerate(reduce_two(h)):
            term = got(h, 4 + i)
            total = total + (term if gets is None else jnp.where(gets, term, 0.0))
        gk_ref[:, cols(h, HD)] = total[0].astype(bf16)
        gv_ref[:, cols(h, HD)] = total[1].astype(bf16)

    def first_reduce(h):
        receive(swap(h))
        fill_one(h)
        sent(gather_one(h) + gather_two(h))
        start(reduce_one(h))

    def second_reduce(h):
        receive(reduce_one(h))
        fill_two(h)
        start(reduce_two(h))

    def store(h, i):
        ref, out = ((att_ref, att_hbm), (dq_ref, dq_hbm))[i]
        c = cols(h, WIDE)
        return pltpu.make_async_copy(ref.at[:, c], out.at[:, c], loc_sem.at[1 + 2 * h + i])

    def head(h, carry):
        receive(share_one(h) + share_two(h))
        c = cols(h, WIDE)

        @pl.when(h == 3)
        def _():
            second_reduce(0)

        def tiles(i):
            chosen = kv[h, 1, 0, i]
            for other in range(2, TREE - 1):
                chosen = jnp.where(parent == other, kv[h, other % 2, other // 2, i], chosen)
            return jnp.concatenate(
                [kv[h, core, y * 2 + z // 2, i], kv[h, 0, 0, i], chosen], 0
            )

        key = tiles(0)
        value = tiles(1)
        s = dot(key, qT[:, c])
        so = s[:TILE] + jnp.concatenate([bias[0]] * 8, 1)
        sr = s[TILE : 2 * TILE]
        sp = s[2 * TILE :] + jnp.concatenate([bias[1]] * 8, 1)
        m = (
            jnp.maximum(
                jnp.maximum(jnp.max(so, 0, keepdims=True), jnp.max(sp, 0, keepdims=True)),
                jnp.max(sr, 0, keepdims=True) - root_off,
            )
            * LOG2
        )
        eo = jnp.exp2(so * LOG2 - m)
        er = jnp.exp2(sr * LOG2 - (m + root_off))
        ep = jnp.exp2(sp * LOG2 - m)
        inv = jnp.where(seen, 1.0 / jnp.sum(eo + er + ep, 0, keepdims=True), 0.0)
        e = jnp.concatenate([eo, er, ep], 0).astype(bf16)
        o = dot(value.T, e) * inv
        d = doT[:, c]
        delta = jnp.sum(o * d.astype(f32), 0, keepdims=True)
        o = o.T
        for i in range(8):
            att_ref[:, cols(h * 8 + i, HD)] = o[i * HD : (i + 1) * HD].astype(bf16)
        store(h, 0).start()

        @pl.when(h < 2)
        def _():
            receive(gather_one(h + 2))
            start(gather_two(h + 2) + share_one(h + 2))

        @pl.when(h > 0)
        def _():
            first_reduce(h - 1)

        @pl.when(h < 3)
        def _():
            receive(gather_two(h + 1))
            start(share_two(h + 1))

        ds = (e.astype(f32) * (dot(value, d) - delta)).astype(bf16)
        dk = dot_nt(ds, (qT[:, c].astype(f32) * inv).astype(bf16)) * (adv * SCALE)
        dv = dot_nt(e, (d.astype(f32) * inv).astype(bf16)) * adv
        for i, place_ in enumerate((2, 0, 1)):
            mine[h, place_, 0] = dk[i * TILE : (i + 1) * TILE].astype(bf16)
            mine[h, place_, 1] = dv[i * TILE : (i + 1) * TILE].astype(bf16)
        start(swap(h))
        g = (dot(key.T, ds) * (inv * (adv * SCALE))).T
        for i in range(8):
            dq_ref[:, cols(h * 8 + i, HD)] = g[i * HD : (i + 1) * HD].astype(bf16)
        store(h, 1).start()
        return carry

    lax.fori_loop(0, KVH, head, 0)

    second_reduce(1)
    first_reduce(3)
    second_reduce(2)
    receive(reduce_two(0))
    close(0)
    second_reduce(3)
    for h in range(1, KVH):
        receive(reduce_two(h))
        close(h)
    stores = [
        pltpu.make_async_copy(gk_ref, gk_hbm, loc_sem.at[9]),
        pltpu.make_async_copy(gv_ref, gv_hbm, loc_sem.at[10]),
    ]
    for copy in stores:
        copy.start()
    for copy in stores + [store_adv] + [store(h, i) for h in range(KVH) for i in range(2)]:
        copy.wait()
    sent(more)

    def drain(h, carry):
        sent(share_one(h) + share_two(h) + swap(h) + reduce_one(h) + reduce_two(h))
        return carry

    lax.fori_loop(0, KVH, drain, 0)


def finish(*refs):
    ins, outs, bufs, adv_out = refs[:5], refs[5:9], refs[10:15], refs[9]
    arrive, leave = refs[15], refs[16]
    loads = [pltpu.make_async_copy(ins[i], bufs[i], arrive.at[i]) for i in range(5)]
    stores = [pltpu.make_async_copy(bufs[i], outs[i], leave.at[i]) for i in range(4)]
    for copy in loads:
        copy.start()
    for load, copy in zip(loads, stores):
        load.wait()
        copy.start()
    loads[4].wait()
    adv_out[0] = bufs[4][0, 0]
    for copy in stores:
        copy.wait()


def body(queries, keys, values, d_out, lengths, ancestors, rewards, pruned, branch_group):
    hbm = pl.BlockSpec(memory_space=pl.ANY)
    dma = pltpu.SemaphoreType.DMA
    wide = jax.ShapeDtypeStruct((HALF, H * HD), bf16)
    narrow = jax.ShapeDtypeStruct((HALF, KVH * HD), bf16)
    i32 = jnp.int32
    results = pl.pallas_call(
        kernel,
        out_shape=(wide, wide, narrow, narrow, jax.ShapeDtypeStruct((8, 128), f32)),
        in_specs=[hbm] * 9,
        out_specs=(hbm,) * 5,
        scratch_shapes=[
            pltpu.VMEM((HALF, H * HD), bf16),
            pltpu.VMEM((HALF, H * HD), bf16),
            pltpu.VMEM((HALF, H * HD), bf16),
            pltpu.VMEM((HALF, H * HD), bf16),
            pltpu.VMEM((HALF, KVH * HD), bf16),
            pltpu.VMEM((HALF, KVH * HD), bf16),
            pltpu.VMEM((8, 128), f32),
            pltpu.SMEM(lengths.shape, i32),
            pltpu.SMEM(ancestors.shape, i32),
            pltpu.SMEM((1,), f32),
            pltpu.SMEM((1,), i32),
            pltpu.SMEM((1,), i32),
            pltpu.VMEM((KVH, 2, 4, 2, TILE, HD), bf16),
            pltpu.VMEM((HD, H * HALF), bf16),
            pltpu.VMEM((HD, H * HALF), bf16),
            pltpu.VMEM((2, TILE, HALF), f32),
            pltpu.VMEM((8, 8, 128), f32),
            pltpu.VMEM((8, 8, 128), f32),
            pltpu.VMEM((KVH, 3, 2, TILE, HD), bf16),
            pltpu.VMEM((KVH, 2, 2, TILE, HD), bf16),
            pltpu.VMEM((KVH, 8, 2, HALF, HD), bf16),
            pltpu.VMEM((KVH, 8, 2, HALF, HD), bf16),
            dma((15,)),
            dma((32,)),
            dma((32,)),
            dma((12,)),
            dma((12,)),
            dma((8,)),
            dma((15,)),
            dma((32,)),
        ],
        compiler_params=pltpu.CompilerParams(
            collective_id=0, has_side_effects=True, vmem_limit_bytes=56 << 20
        ),
        name="tree_attention",
    )(queries, keys, values, d_out, lengths, ancestors, rewards, pruned, branch_group)
    return pl.pallas_call(
        finish,
        out_shape=(wide, wide, narrow, narrow, jax.ShapeDtypeStruct((1,), f32)),
        in_specs=[hbm] * 5,
        out_specs=(hbm,) * 4 + (pl.BlockSpec(memory_space=pltpu.SMEM),),
        scratch_shapes=[pltpu.VMEM(a.shape, a.dtype) for a in results] + [dma((5,)), dma((4,))],
        name="finish",
    )(*results)


def solution(mesh):
    rows = P(("ctx", "tp"), None)
    in_specs = (rows, rows, rows, rows, P(), P("ctx", None), P("ctx"), P("ctx"), P("ctx"))
    out_specs = (rows, rows, rows, rows, P("ctx"))
    return jax.shard_map(body, mesh=mesh, in_specs=in_specs, out_specs=out_specs, check_vma=False)
```

```python
import jax
import jax.numpy as jnp
from jax import lax
from jax.experimental import pallas as pl
from jax.experimental.pallas import tpu as pltpu
from jax.sharding import PartitionSpec as P

H = 32
KVH = 4
HD = 128
TILE = 256
HALF = 128
TREE = 8
GROUPS = 8
WIDE = 1024
MESH = pl.DeviceIdType.MESH
SCALE = HD**-0.5
LOG2 = SCALE * 1.4426950408889634
NEG = -1e30
f32 = jnp.float32
bf16 = jnp.bfloat16
NT = (((1,), (1,)), ((), ()))
SPLIT = 64


def cols(index, size):
    return pl.ds(pl.multiple_of(index * size, size), size)


def dot(a, b):
    return jnp.dot(a, b, preferred_element_type=f32)


def dot_nt(a, b):
    return lax.dot_general(a, b, NT, preferred_element_type=f32)


def kernel(
    q_hbm, k_hbm, v_hbm, do_hbm, len_hbm, anc_hbm, rew_hbm, pru_hbm, grp_hbm,
    att_hbm, dq_hbm, gk_hbm, gv_hbm, adv_hbm,
    q_ref, do_ref, att_ref, dq_ref, gk_ref, gv_ref, adv_ref,
    len_ref, anc_ref, rew_ref, pru_ref, grp_ref,
    kv, qT, doT, bias, near, far, mine, theirs, inbox, outbox,
    loc_sem, ag_send, ag_recv, core_send, core_recv, st_send, st_recv, rs_recv,
):
    ctx = lax.axis_index("ctx")
    tp = lax.axis_index("tp")
    tree = ctx // TREE
    seg = ctx % TREE
    core = ctx % 2
    z = ((ctx // 2) % 2) * 2 + tp
    y = (ctx // 4) % 2
    first = tree * TREE

    def place(yy, zz, cc):
        zz = zz % 4
        return first + yy * 4 + (zz // 2) * 2 + cc, zz % 2

    dev_core = place(y, z, 1 - core)
    pair = z + 1 - 2 * (z % 2)
    side = z + 3 + 2 * (z % 2)
    dev_pair = place(y, pair, core)
    dev_side = place(y, side, core)
    dev_far = place(y, z + 2, core)
    dev_y = place(1 - y, z, core)
    kin = [(first + (seg + i) % TREE, tp) for i in range(1, TREE)]
    others = [(((tree + i) % 8) * TREE + seg, tp) for i in range(1, 8)]

    barrier = pltpu.get_barrier_semaphore()
    for device in kin + [dev_pair, dev_side] + others:
        pl.semaphore_signal(barrier, inc=1, device_id=device, device_id_type=MESH)

    small = [
        pltpu.make_async_copy(a, b, loc_sem.at[i])
        for i, (a, b) in enumerate(
            zip(
                (len_hbm, anc_hbm, rew_hbm, pru_hbm, grp_hbm),
                (len_ref, anc_ref, rew_ref, pru_ref, grp_ref),
            )
        )
    ]
    rows_here = pl.ds(tp * HALF, HALF)
    large = [
        pltpu.make_async_copy(q_hbm, q_ref, loc_sem.at[5]),
        pltpu.make_async_copy(do_hbm, do_ref, loc_sem.at[6]),
    ]
    own_kv = []
    for h in range(KVH):
        for i, ref in enumerate((k_hbm, v_hbm)):
            own_kv.append(
                pltpu.make_async_copy(
                    ref.at[:, pl.ds(h * HD, HD)],
                    kv.at[h, core, y * 2 + z // 2, i, rows_here],
                    loc_sem.at[7 + 2 * h + i],
                )
            )
    for copy in small + large + own_kv:
        copy.start()
    for copy in small:
        copy.wait()

    lane = lax.broadcasted_iota(jnp.int32, (8, 128), 1)
    row = lax.broadcasted_iota(jnp.int32, (8, 128), 0)
    reward = rew_ref[0]
    living = 1.0 - pru_ref[0].astype(f32)
    belongs = lane == grp_ref[0]
    parent = jnp.int32(0)
    for o in range(1, TREE):
        parent = parent + jnp.where(o < seg, anc_ref[0, o - 1] * (seg - o), 0)
    has_parent = parent > 0
    terms = jnp.where(
        row == 0, living, jnp.where(row == 1, living * reward, living * reward * reward)
    )
    near[0] = jnp.where(
        row < 3, jnp.where(belongs, terms, 0.0), jnp.where(has_parent, parent, -1).astype(f32)
    )

    for copy in own_kv:
        copy.wait()
    pl.semaphore_wait(barrier, 16)

    def remote(src, dst, device, sends, recvs, i):
        return pltpu.make_async_remote_copy(
            src_ref=src, dst_ref=dst, send_sem=sends.at[i], recv_sem=recvs.at[i],
            device_id=device, device_id_type=MESH,
        )

    def act(method, moves, which):
        for move in moves:
            operation = getattr(move[0], method)
            if move[which] is None:
                operation()
            else:
                pl.when(move[which])(operation)

    def start(moves):
        act("start", moves, 1)

    def receive(moves):
        act("wait_recv", moves, 2)

    def sent(moves):
        act("wait_send", moves, 1)

    lower = y == 0
    upper = y == 1

    def block(h, yy, zz, begin=0, size=HALF):
        zz = zz % 4
        return kv.at[
            h, core, yy * 2 + zz // 2, :, pl.ds(pl.multiple_of((zz % 2) * HALF + begin, 16), size)
        ]

    def gather(h, pieces, base):
        return [
            (remote(ref, ref, device, ag_send, ag_recv, h * 8 + base + i), sends, gets)
            for i, (ref, device, sends, gets) in enumerate(pieces)
        ]

    def gather_one(h):
        here = block(h, y, z)
        return gather(
            h,
            [
                (here, dev_pair, None, None),
                (here, dev_side, lower | (z < 2), lower | (z >= 2)),
                (here, dev_y, lower, upper),
                (here, dev_far, lower | (z < 2), lower | (z >= 2)),
            ],
            0,
        )

    def gather_two(h):
        rest = HALF - SPLIT
        return gather(
            h,
            [
                (block(h, 1 - y, z), dev_pair, upper, upper),
                (block(h, 1 - y, z, 0, SPLIT), dev_side, upper, upper),
                (block(h, y, side, SPLIT, rest), dev_y, lower, upper),
                (block(h, y, z + 2), dev_y, lower, upper),
            ],
            4,
        )

    def share(h, yy, i, needed):
        ref = kv.at[h, core, pl.ds(yy * 2, 2)]
        return [(remote(ref, ref, dev_core, core_send, core_recv, h * 3 + i), needed, needed)]

    def share_one(h):
        return share(h, y, 0, None)

    def share_two(h):
        return share(h, 1 - y, 1, upper)

    notes = [
        (remote(near.at[0], near.at[i], kin[i - 1], st_send, st_recv, i), None, None)
        for i in range(1, TREE)
    ]
    more = [
        (
            pltpu.make_async_remote_copy(
                src_ref=far.at[0], dst_ref=far.at[i], send_sem=st_send.at[i],
                recv_sem=st_recv.at[7 + i], device_id=others[i - 1], device_id_type=MESH,
            ),
            None,
            None,
        )
        for i in range(1, 8)
    ]

    start(gather_one(0))
    start(notes)
    start(gather_one(1))

    own_len = len_ref[ctx]
    par_len = jnp.where(has_parent, len_ref[first + parent], 0)
    u = lax.broadcasted_iota(jnp.int32, (TILE, HALF), 0)
    t = lax.broadcasted_iota(jnp.int32, (TILE, HALF), 1) + tp * HALF
    bias[0] = jnp.where((u <= t) & (u < own_len), 0.0, NEG)
    bias[1] = jnp.where(u < par_len, 0.0, NEG)
    root_off = jnp.where(seg > 0, 0.0, -NEG)
    slot = lax.broadcasted_iota(jnp.int32, (1, WIDE), 1) % HALF + tp * HALF
    seen = slot < own_len
    for copy in large:
        copy.wait()

    def turn(h, carry):
        qT[:, cols(h, HD)] = q_ref[:, cols(h, HD)].T
        doT[:, cols(h, HD)] = do_ref[:, cols(h, HD)].T
        return carry

    lax.fori_loop(0, H, turn, 0, unroll=4)

    receive(gather_one(0))
    start(gather_two(0) + share_one(0) + gather_one(2))
    receive(notes)
    summed = near[0]
    for i in range(1, TREE):
        summed = summed + near[i]
    far[0] = summed
    mate = jnp.where(core == 0, near[7], near[1])[3:4, 0:1]
    sent(notes)
    start(more)
    receive(gather_one(1))
    start(gather_two(1) + share_one(1) + gather_one(3))
    receive(gather_two(0))
    start(share_two(0))
    receive(more)
    summed = far[0]
    for i in range(1, 8):
        summed = summed + far[i]
    members = jnp.maximum(summed[0:1], 1.0)
    average = summed[1:2] / members
    spread = jnp.sqrt(jnp.maximum(summed[2:3] / members - average * average, 0.0))
    here = belongs[0:1]
    adv = (
        living
        * (reward - jnp.sum(jnp.where(here, average, 0.0), 1, keepdims=True))
        / jnp.sum(jnp.where(here, jnp.maximum(spread, 1.0), 0.0), 1, keepdims=True)
    )
    adv_ref[...] = jnp.broadcast_to(adv, (8, 128))
    store_adv = pltpu.make_async_copy(adv_ref, adv_hbm, loc_sem.at[0])
    store_adv.start()

    def swap(h):
        copy = remote(
            mine.at[h, pl.ds(0, 2)], theirs.at[h], dev_core, core_send, core_recv, h * 3 + 2
        )
        return [(copy, None, None)]

    parent_mark = jnp.where(has_parent, parent, -1)

    def part(h, yy, zz, begin=0, size=HALF):
        zz = zz % 4
        target = yy * 4 + (zz // 2) * 2 + core
        rows = pl.ds(pl.multiple_of((zz % 2) * HALF + begin, 16), size)
        own_w = jnp.where(parent_mark == target, 1.0, 0.0)
        mate_w = jnp.where(mate == target.astype(f32), 1.0, 0.0)
        root_w = jnp.where(target == 0, 1.0, 0.0)
        return (
            mine[h, 1, :, rows].astype(f32) * own_w
            + theirs[h, 1, :, rows].astype(f32) * mate_w[None]
            + (mine[h, 0, :, rows].astype(f32) + theirs[h, 0, :, rows].astype(f32)) * root_w
        )

    def own_part(h, zz):
        rows = pl.ds(pl.multiple_of((zz % 2) * HALF, HALF), HALF)
        return mine[h, 2, :, rows].astype(f32)

    low = pl.ds(0, SPLIT)
    high = pl.ds(SPLIT, HALF - SPLIT)
    whole = pl.ds(0, HALF)

    def ship(h, i, rows, device, sends, gets):
        copy = remote(
            outbox.at[h, i, :, rows], inbox.at[h, i, :, rows], device, ag_send, rs_recv, h * 8 + i
        )
        return copy, sends, gets

    def reduce_one(h):
        return [
            ship(h, 0, whole, dev_pair, upper, upper),
            ship(h, 1, low, dev_side, upper, upper),
            ship(h, 2, high, dev_y, upper, lower),
            ship(h, 3, whole, dev_y, upper, lower),
        ]

    def reduce_two(h):
        return [
            ship(h, 4, whole, dev_y, upper, lower),
            ship(h, 5, whole, dev_pair, None, None),
            ship(h, 6, whole, dev_side, lower | (z >= 2), lower | (z < 2)),
            ship(h, 7, whole, dev_far, lower | (z >= 2), lower | (z < 2)),
        ]

    def fill_one(h):
        @pl.when(upper)
        def _():
            outbox[h, 0] = part(h, 1 - y, pair).astype(bf16)
            beside = part(h, 1 - y, side).astype(bf16)
            outbox[h, 1, :, low] = beside[:, :SPLIT]
            outbox[h, 2, :, high] = beside[:, SPLIT:]
            outbox[h, 3] = part(h, 1 - y, z + 2).astype(bf16)

    def got(h, i, rows=whole):
        return inbox[h, i, :, rows].astype(f32)

    def fill_two(h):
        outbox[h, 5] = (part(h, y, pair) + own_part(h, pair)).astype(bf16)

        @pl.when(upper)
        def _():
            over = part(h, 1 - y, z) + got(h, 0)
            outbox[h, 4, :, low] = (over[:, :SPLIT] + got(h, 1, low)).astype(bf16)
            outbox[h, 4, :, high] = over[:, SPLIT:].astype(bf16)
            outbox[h, 6] = part(h, y, side).astype(bf16)
            outbox[h, 7] = part(h, y, z + 2).astype(bf16)

        @pl.when(lower)
        def _():
            beside = part(h, y, side)
            outbox[h, 6, :, low] = beside[:, :SPLIT].astype(bf16)
            outbox[h, 6, :, high] = (beside[:, SPLIT:] + got(h, 2, high)).astype(bf16)
            outbox[h, 7] = (part(h, y, z + 2) + got(h, 3)).astype(bf16)

    def close(h):
        total = part(h, y, z) + own_part(h, z)
        for i, (_, _, gets) in enumerate(reduce_two(h)):
            term = got(h, 4 + i)
            total = total + (term if gets is None else jnp.where(gets, term, 0.0))
        gk_ref[:, cols(h, HD)] = total[0].astype(bf16)
        gv_ref[:, cols(h, HD)] = total[1].astype(bf16)

    def first_reduce(h):
        receive(swap(h))
        fill_one(h)
        sent(gather_one(h) + gather_two(h))
        start(reduce_one(h))

    def second_reduce(h):
        receive(reduce_one(h))
        fill_two(h)
        start(reduce_two(h))

    def store(h, i):
        ref, out = ((att_ref, att_hbm), (dq_ref, dq_hbm))[i]
        c = cols(h, WIDE)
        return pltpu.make_async_copy(ref.at[:, c], out.at[:, c], loc_sem.at[1 + 2 * h + i])

    def head(h, carry):
        receive(share_one(h) + share_two(h))
        c = cols(h, WIDE)

        @pl.when(h == 3)
        def _():
            second_reduce(0)

        def tiles(i):
            chosen = kv[h, 1, 0, i]
            for other in range(2, TREE - 1):
                chosen = jnp.where(parent == other, kv[h, other % 2, other // 2, i], chosen)
            return jnp.concatenate(
                [kv[h, core, y * 2 + z // 2, i], kv[h, 0, 0, i], chosen], 0
            )

        key = tiles(0)
        value = tiles(1)
        s = dot(key, qT[:, c])
        so = s[:TILE] + jnp.concatenate([bias[0]] * 8, 1)
        sr = s[TILE : 2 * TILE]
        sp = s[2 * TILE :] + jnp.concatenate([bias[1]] * 8, 1)
        m = (
            jnp.maximum(
                jnp.maximum(jnp.max(so, 0, keepdims=True), jnp.max(sp, 0, keepdims=True)),
                jnp.max(sr, 0, keepdims=True) - root_off,
            )
            * LOG2
        )
        eo = jnp.exp2(so * LOG2 - m)
        er = jnp.exp2(sr * LOG2 - (m + root_off))
        ep = jnp.exp2(sp * LOG2 - m)
        inv = jnp.where(seen, 1.0 / jnp.sum(eo + er + ep, 0, keepdims=True), 0.0)
        e = jnp.concatenate([eo, er, ep], 0).astype(bf16)
        o = dot(value.T, e) * inv
        d = doT[:, c]
        delta = jnp.sum(o * d.astype(f32), 0, keepdims=True)
        o = o.T
        for i in range(8):
            att_ref[:, cols(h * 8 + i, HD)] = o[i * HD : (i + 1) * HD].astype(bf16)
        store(h, 0).start()

        @pl.when(h < 2)
        def _():
            receive(gather_one(h + 2))
            start(gather_two(h + 2) + share_one(h + 2))

        @pl.when(h > 0)
        def _():
            first_reduce(h - 1)

        @pl.when(h < 3)
        def _():
            receive(gather_two(h + 1))
            start(share_two(h + 1))

        ds = (e.astype(f32) * (dot(value, d) - delta)).astype(bf16)
        dk = dot_nt(ds, (qT[:, c].astype(f32) * inv).astype(bf16)) * (adv * SCALE)
        dv = dot_nt(e, (d.astype(f32) * inv).astype(bf16)) * adv
        for i, place_ in enumerate((2, 0, 1)):
            mine[h, place_, 0] = dk[i * TILE : (i + 1) * TILE].astype(bf16)
            mine[h, place_, 1] = dv[i * TILE : (i + 1) * TILE].astype(bf16)
        start(swap(h))
        g = (dot(key.T, ds) * (inv * (adv * SCALE))).T
        for i in range(8):
            dq_ref[:, cols(h * 8 + i, HD)] = g[i * HD : (i + 1) * HD].astype(bf16)
        store(h, 1).start()
        return carry

    lax.fori_loop(0, KVH, head, 0)

    second_reduce(1)
    first_reduce(3)
    second_reduce(2)
    receive(reduce_two(0))
    close(0)
    second_reduce(3)
    for h in (1, 2):
        receive(reduce_two(h))
        close(h)
    sent(more)
    store_adv.wait()

    def drain(h, carry):
        sent(share_one(h) + share_two(h) + swap(h) + reduce_one(h))
        pl.when(h < 3)(lambda: sent(reduce_two(h)))
        for i in range(2):
            store(h, i).wait()
        return carry

    lax.fori_loop(0, KVH, drain, 0)
    receive(reduce_two(3))
    close(3)
    stores = [
        pltpu.make_async_copy(gk_ref, gk_hbm, loc_sem.at[9]),
        pltpu.make_async_copy(gv_ref, gv_hbm, loc_sem.at[10]),
    ]
    for copy in stores:
        copy.start()
    sent(reduce_two(3))
    for copy in stores:
        copy.wait()


def finish(*refs):
    ins, outs, bufs, adv_out = refs[:5], refs[5:9], refs[10:15], refs[9]
    arrive, leave = refs[15], refs[16]
    loads, stores = [], []
    for i, pieces in enumerate((4, 4, 1, 1)):
        size = HALF // pieces
        for p in range(pieces):
            rows = pl.ds(p * size, size)
            n = len(loads)
            loads.append(pltpu.make_async_copy(ins[i].at[rows], bufs[i].at[rows], arrive.at[n]))
            stores.append(pltpu.make_async_copy(bufs[i].at[rows], outs[i].at[rows], leave.at[n]))
    last = pltpu.make_async_copy(ins[4], bufs[4], arrive.at[10])
    last.start()
    for copy in loads:
        copy.start()
    for load, copy in zip(loads, stores):
        load.wait()
        copy.start()
    last.wait()
    adv_out[0] = bufs[4][0, 0]
    for copy in stores:
        copy.wait()


def body(queries, keys, values, d_out, lengths, ancestors, rewards, pruned, branch_group):
    hbm = pl.BlockSpec(memory_space=pl.ANY)
    dma = pltpu.SemaphoreType.DMA
    wide = jax.ShapeDtypeStruct((HALF, H * HD), bf16)
    narrow = jax.ShapeDtypeStruct((HALF, KVH * HD), bf16)
    i32 = jnp.int32
    results = pl.pallas_call(
        kernel,
        out_shape=(wide, wide, narrow, narrow, jax.ShapeDtypeStruct((8, 128), f32)),
        in_specs=[hbm] * 9,
        out_specs=(hbm,) * 5,
        scratch_shapes=[
            pltpu.VMEM((HALF, H * HD), bf16),
            pltpu.VMEM((HALF, H * HD), bf16),
            pltpu.VMEM((HALF, H * HD), bf16),
            pltpu.VMEM((HALF, H * HD), bf16),
            pltpu.VMEM((HALF, KVH * HD), bf16),
            pltpu.VMEM((HALF, KVH * HD), bf16),
            pltpu.VMEM((8, 128), f32),
            pltpu.SMEM(lengths.shape, i32),
            pltpu.SMEM(ancestors.shape, i32),
            pltpu.SMEM((1,), f32),
            pltpu.SMEM((1,), i32),
            pltpu.SMEM((1,), i32),
            pltpu.VMEM((KVH, 2, 4, 2, TILE, HD), bf16),
            pltpu.VMEM((HD, H * HALF), bf16),
            pltpu.VMEM((HD, H * HALF), bf16),
            pltpu.VMEM((2, TILE, HALF), f32),
            pltpu.VMEM((8, 8, 128), f32),
            pltpu.VMEM((8, 8, 128), f32),
            pltpu.VMEM((KVH, 3, 2, TILE, HD), bf16),
            pltpu.VMEM((KVH, 2, 2, TILE, HD), bf16),
            pltpu.VMEM((KVH, 8, 2, HALF, HD), bf16),
            pltpu.VMEM((KVH, 8, 2, HALF, HD), bf16),
            dma((15,)),
            dma((32,)),
            dma((32,)),
            dma((12,)),
            dma((12,)),
            dma((8,)),
            dma((15,)),
            dma((32,)),
        ],
        compiler_params=pltpu.CompilerParams(
            collective_id=0, has_side_effects=True, vmem_limit_bytes=56 << 20
        ),
        name="tree_attention",
    )(queries, keys, values, d_out, lengths, ancestors, rewards, pruned, branch_group)
    return pl.pallas_call(
        finish,
        out_shape=(wide, wide, narrow, narrow, jax.ShapeDtypeStruct((1,), f32)),
        in_specs=[hbm] * 5,
        out_specs=(hbm,) * 4 + (pl.BlockSpec(memory_space=pltpu.SMEM),),
        scratch_shapes=[pltpu.VMEM(a.shape, a.dtype) for a in results] + [dma((11,)), dma((10,))],
        name="finish",
    )(*results)


def solution(mesh):
    rows = P(("ctx", "tp"), None)
    in_specs = (rows, rows, rows, rows, P(), P("ctx", None), P("ctx"), P("ctx"), P("ctx"))
    out_specs = (rows, rows, rows, rows, P("ctx"))
    return jax.shard_map(body, mesh=mesh, in_specs=in_specs, out_specs=out_specs, check_vma=False)
```

```python
import jax
import jax.numpy as jnp
from jax import lax
from jax.experimental import pallas as pl
from jax.experimental.pallas import tpu as pltpu
from jax.sharding import PartitionSpec as P

H = 32
KVH = 4
HD = 128
TILE = 256
HALF = 128
TREE = 8
GROUPS = 8
WIDE = 1024
MESH = pl.DeviceIdType.MESH
SCALE = HD**-0.5
LOG2 = SCALE * 1.4426950408889634
NEG = -1e30
f32 = jnp.float32
bf16 = jnp.bfloat16
NT = (((1,), (1,)), ((), ()))
SPLIT = 64


def cols(index, size):
    return pl.ds(pl.multiple_of(index * size, size), size)


def dot(a, b):
    return jnp.dot(a, b, preferred_element_type=f32)


def dot_nt(a, b):
    return lax.dot_general(a, b, NT, preferred_element_type=f32)


def kernel(
    q_hbm, k_hbm, v_hbm, do_hbm, len_hbm, anc_hbm, rew_hbm, pru_hbm, grp_hbm,
    att_hbm, dq_hbm, gk_hbm, gv_hbm, adv_hbm,
    q_ref, do_ref, att_ref, dq_ref, gk_ref, gv_ref, adv_ref,
    len_ref, anc_ref, rew_ref, pru_ref, grp_ref,
    kv, qT, doT, bias, near, far, mine, theirs, inbox, outbox,
    loc_sem, ag_send, ag_recv, core_send, core_recv, st_send, st_recv, rs_recv,
):
    ctx = lax.axis_index("ctx")
    tp = lax.axis_index("tp")
    tree = ctx // TREE
    seg = ctx % TREE
    core = ctx % 2
    z = ((ctx // 2) % 2) * 2 + tp
    y = (ctx // 4) % 2
    first = tree * TREE

    def place(yy, zz, cc):
        zz = zz % 4
        return first + yy * 4 + (zz // 2) * 2 + cc, zz % 2

    dev_core = place(y, z, 1 - core)
    pair = z + 1 - 2 * (z % 2)
    side = z + 3 + 2 * (z % 2)
    dev_pair = place(y, pair, core)
    dev_side = place(y, side, core)
    dev_far = place(y, z + 2, core)
    dev_y = place(1 - y, z, core)
    kin = [(first + (seg + i) % TREE, tp) for i in range(1, TREE)]
    others = [(((tree + i) % 8) * TREE + seg, tp) for i in range(1, 8)]

    barrier = pltpu.get_barrier_semaphore()
    for device in kin + [dev_pair, dev_side] + others:
        pl.semaphore_signal(barrier, inc=1, device_id=device, device_id_type=MESH)

    small = [
        pltpu.make_async_copy(a, b, loc_sem.at[i])
        for i, (a, b) in enumerate(
            zip(
                (len_hbm, anc_hbm, rew_hbm, pru_hbm, grp_hbm),
                (len_ref, anc_ref, rew_ref, pru_ref, grp_ref),
            )
        )
    ]
    rows_here = pl.ds(tp * HALF, HALF)
    large = [
        pltpu.make_async_copy(q_hbm, q_ref, loc_sem.at[5]),
        pltpu.make_async_copy(do_hbm, do_ref, loc_sem.at[6]),
    ]
    own_kv = []
    for h in range(KVH):
        for i, ref in enumerate((k_hbm, v_hbm)):
            own_kv.append(
                pltpu.make_async_copy(
                    ref.at[:, pl.ds(h * HD, HD)],
                    kv.at[h, core, y * 2 + z // 2, i, rows_here],
                    loc_sem.at[7 + 2 * h + i],
                )
            )
    for copy in small + large + own_kv:
        copy.start()
    for copy in small:
        copy.wait()

    lane = lax.broadcasted_iota(jnp.int32, (8, 128), 1)
    row = lax.broadcasted_iota(jnp.int32, (8, 128), 0)
    reward = rew_ref[0]
    living = 1.0 - pru_ref[0].astype(f32)
    belongs = lane == grp_ref[0]
    parent = jnp.int32(0)
    for o in range(1, TREE):
        parent = parent + jnp.where(o < seg, anc_ref[0, o - 1] * (seg - o), 0)
    has_parent = parent > 0
    terms = jnp.where(
        row == 0, living, jnp.where(row == 1, living * reward, living * reward * reward)
    )
    near[0] = jnp.where(
        row < 3, jnp.where(belongs, terms, 0.0), jnp.where(has_parent, parent, -1).astype(f32)
    )

    for copy in own_kv:
        copy.wait()
    pl.semaphore_wait(barrier, 16)

    def remote(src, dst, device, sends, recvs, i):
        return pltpu.make_async_remote_copy(
            src_ref=src, dst_ref=dst, send_sem=sends.at[i], recv_sem=recvs.at[i],
            device_id=device, device_id_type=MESH,
        )

    def act(method, moves, which):
        for move in moves:
            operation = getattr(move[0], method)
            if move[which] is None:
                operation()
            else:
                pl.when(move[which])(operation)

    def start(moves):
        act("start", moves, 1)

    def receive(moves):
        act("wait_recv", moves, 2)

    def sent(moves):
        act("wait_send", moves, 1)

    lower = y == 0
    upper = y == 1

    def block(h, yy, zz, begin=0, size=HALF):
        zz = zz % 4
        return kv.at[
            h, core, yy * 2 + zz // 2, :, pl.ds(pl.multiple_of((zz % 2) * HALF + begin, 16), size)
        ]

    def gather(h, pieces, base):
        return [
            (remote(ref, ref, device, ag_send, ag_recv, h * 8 + base + i), sends, gets)
            for i, (ref, device, sends, gets) in enumerate(pieces)
        ]

    def gather_one(h):
        here = block(h, y, z)
        return gather(
            h,
            [
                (here, dev_pair, None, None),
                (here, dev_side, lower | (z < 2), lower | (z >= 2)),
                (here, dev_y, lower, upper),
                (here, dev_far, lower | (z < 2), lower | (z >= 2)),
            ],
            0,
        )

    def gather_two(h):
        rest = HALF - SPLIT
        return gather(
            h,
            [
                (block(h, 1 - y, z), dev_pair, upper, upper),
                (block(h, 1 - y, z, 0, SPLIT), dev_side, upper, upper),
                (block(h, y, side, SPLIT, rest), dev_y, lower, upper),
                (block(h, y, z + 2), dev_y, lower, upper),
            ],
            4,
        )

    def share(h, yy, i, needed):
        ref = kv.at[h, core, pl.ds(yy * 2, 2)]
        return [(remote(ref, ref, dev_core, core_send, core_recv, h * 3 + i), needed, needed)]

    def share_one(h):
        return share(h, y, 0, None)

    def share_two(h):
        return share(h, 1 - y, 1, upper)

    notes = [
        (remote(near.at[0], near.at[i], kin[i - 1], st_send, st_recv, i), None, None)
        for i in range(1, TREE)
    ]
    more = [
        (
            pltpu.make_async_remote_copy(
                src_ref=far.at[0], dst_ref=far.at[i], send_sem=st_send.at[i],
                recv_sem=st_recv.at[7 + i], device_id=others[i - 1], device_id_type=MESH,
            ),
            None,
            None,
        )
        for i in range(1, 8)
    ]

    start(gather_one(0))
    start(notes)
    start(gather_one(1))

    own_len = len_ref[ctx]
    par_len = jnp.where(has_parent, len_ref[first + parent], 0)
    u = lax.broadcasted_iota(jnp.int32, (TILE, HALF), 0)
    t = lax.broadcasted_iota(jnp.int32, (TILE, HALF), 1) + tp * HALF
    bias[0] = jnp.where((u <= t) & (u < own_len), 0.0, NEG)
    bias[1] = jnp.where(u < par_len, 0.0, NEG)
    root_off = jnp.where(seg > 0, 0.0, -NEG)
    slot = lax.broadcasted_iota(jnp.int32, (1, WIDE), 1) % HALF + tp * HALF
    seen = slot < own_len
    for copy in large:
        copy.wait()

    def turn(h, carry):
        qT[:, cols(h, HD)] = q_ref[:, cols(h, HD)].T
        doT[:, cols(h, HD)] = do_ref[:, cols(h, HD)].T
        return carry

    lax.fori_loop(0, H, turn, 0, unroll=4)

    receive(gather_one(0))
    start(gather_two(0) + share_one(0) + gather_one(2))
    receive(notes)
    summed = near[0]
    for i in range(1, TREE):
        summed = summed + near[i]
    far[0] = summed
    mate = jnp.where(core == 0, near[7], near[1])[3:4, 0:1]
    sent(notes)
    start(more)
    receive(gather_one(1))
    start(gather_two(1) + share_one(1) + gather_one(3))
    receive(gather_two(0))
    start(share_two(0))
    receive(more)
    summed = far[0]
    for i in range(1, 8):
        summed = summed + far[i]
    members = jnp.maximum(summed[0:1], 1.0)
    average = summed[1:2] / members
    spread = jnp.sqrt(jnp.maximum(summed[2:3] / members - average * average, 0.0))
    here = belongs[0:1]
    adv = (
        living
        * (reward - jnp.sum(jnp.where(here, average, 0.0), 1, keepdims=True))
        / jnp.sum(jnp.where(here, jnp.maximum(spread, 1.0), 0.0), 1, keepdims=True)
    )
    adv_ref[...] = jnp.broadcast_to(adv, (8, 128))
    store_adv = pltpu.make_async_copy(adv_ref, adv_hbm, loc_sem.at[0])
    store_adv.start()

    def swap(h):
        copy = remote(
            mine.at[h, pl.ds(0, 2)], theirs.at[h], dev_core, core_send, core_recv, h * 3 + 2
        )
        return [(copy, None, None)]

    parent_mark = jnp.where(has_parent, parent, -1)

    def part(h, yy, zz, begin=0, size=HALF):
        zz = zz % 4
        target = yy * 4 + (zz // 2) * 2 + core
        rows = pl.ds(pl.multiple_of((zz % 2) * HALF + begin, 16), size)
        own_w = jnp.where(parent_mark == target, 1.0, 0.0)
        mate_w = jnp.where(mate == target.astype(f32), 1.0, 0.0)
        root_w = jnp.where(target == 0, 1.0, 0.0)
        return (
            mine[h, 1, :, rows].astype(f32) * own_w
            + theirs[h, 1, :, rows].astype(f32) * mate_w[None]
            + (mine[h, 0, :, rows].astype(f32) + theirs[h, 0, :, rows].astype(f32)) * root_w
        )

    def own_part(h, zz):
        rows = pl.ds(pl.multiple_of((zz % 2) * HALF, HALF), HALF)
        return mine[h, 2, :, rows].astype(f32)

    low = pl.ds(0, SPLIT)
    high = pl.ds(SPLIT, HALF - SPLIT)
    whole = pl.ds(0, HALF)

    def ship(h, i, rows, device, sends, gets):
        copy = remote(
            outbox.at[h, i, :, rows], inbox.at[h, i, :, rows], device, ag_send, rs_recv, h * 8 + i
        )
        return copy, sends, gets

    def reduce_one(h):
        return [
            ship(h, 0, whole, dev_pair, upper, upper),
            ship(h, 1, low, dev_side, upper, upper),
            ship(h, 2, high, dev_y, upper, lower),
            ship(h, 3, whole, dev_y, upper, lower),
        ]

    def reduce_two(h):
        return [
            ship(h, 4, whole, dev_y, upper, lower),
            ship(h, 5, whole, dev_pair, None, None),
            ship(h, 6, whole, dev_side, lower | (z >= 2), lower | (z < 2)),
            ship(h, 7, whole, dev_far, lower | (z >= 2), lower | (z < 2)),
        ]

    def fill_one(h):
        @pl.when(upper)
        def _():
            outbox[h, 0] = part(h, 1 - y, pair).astype(bf16)
            beside = part(h, 1 - y, side).astype(bf16)
            outbox[h, 1, :, low] = beside[:, :SPLIT]
            outbox[h, 2, :, high] = beside[:, SPLIT:]
            outbox[h, 3] = part(h, 1 - y, z + 2).astype(bf16)

    def got(h, i, rows=whole):
        return inbox[h, i, :, rows].astype(f32)

    def fill_two(h):
        outbox[h, 5] = (part(h, y, pair) + own_part(h, pair)).astype(bf16)

        @pl.when(upper)
        def _():
            over = part(h, 1 - y, z) + got(h, 0)
            outbox[h, 4, :, low] = (over[:, :SPLIT] + got(h, 1, low)).astype(bf16)
            outbox[h, 4, :, high] = over[:, SPLIT:].astype(bf16)
            outbox[h, 6] = part(h, y, side).astype(bf16)
            outbox[h, 7] = part(h, y, z + 2).astype(bf16)

        @pl.when(lower)
        def _():
            beside = part(h, y, side)
            outbox[h, 6, :, low] = beside[:, :SPLIT].astype(bf16)
            outbox[h, 6, :, high] = (beside[:, SPLIT:] + got(h, 2, high)).astype(bf16)
            outbox[h, 7] = (part(h, y, z + 2) + got(h, 3)).astype(bf16)

    def close(h):
        total = part(h, y, z) + own_part(h, z)
        for i, (_, _, gets) in enumerate(reduce_two(h)):
            term = got(h, 4 + i)
            total = total + (term if gets is None else jnp.where(gets, term, 0.0))
        gk_ref[:, cols(h, HD)] = total[0].astype(bf16)
        gv_ref[:, cols(h, HD)] = total[1].astype(bf16)

    def first_reduce(h):
        receive(swap(h))
        fill_one(h)
        sent(gather_one(h) + gather_two(h))
        start(reduce_one(h))

    def second_reduce(h):
        receive(reduce_one(h))
        fill_two(h)
        start(reduce_two(h))

    def store(h, i):
        ref, out = ((att_ref, att_hbm), (dq_ref, dq_hbm))[i]
        c = cols(h, WIDE)
        return pltpu.make_async_copy(ref.at[:, c], out.at[:, c], loc_sem.at[1 + 2 * h + i])

    def head(h, carry):
        receive(share_one(h) + share_two(h))
        c = cols(h, WIDE)

        @pl.when(h == 3)
        def _():
            second_reduce(0)

        def tiles(i):
            chosen = kv[h, 1, 0, i]
            for other in range(2, TREE - 1):
                chosen = jnp.where(parent == other, kv[h, other % 2, other // 2, i], chosen)
            return jnp.concatenate(
                [kv[h, core, y * 2 + z // 2, i], kv[h, 0, 0, i], chosen], 0
            )

        key = tiles(0)
        value = tiles(1)
        s = dot(key, qT[:, c])
        so = s[:TILE] + jnp.concatenate([bias[0]] * 8, 1)
        sr = s[TILE : 2 * TILE]
        sp = s[2 * TILE :] + jnp.concatenate([bias[1]] * 8, 1)
        m = (
            jnp.maximum(
                jnp.maximum(jnp.max(so, 0, keepdims=True), jnp.max(sp, 0, keepdims=True)),
                jnp.max(sr, 0, keepdims=True) - root_off,
            )
            * LOG2
        )
        eo = jnp.exp2(so * LOG2 - m)
        er = jnp.exp2(sr * LOG2 - (m + root_off))
        ep = jnp.exp2(sp * LOG2 - m)
        inv = jnp.where(seen, 1.0 / jnp.sum(eo + er + ep, 0, keepdims=True), 0.0)
        e = jnp.concatenate([eo, er, ep], 0).astype(bf16)
        o = dot(value.T, e) * inv
        d = doT[:, c]
        delta = jnp.sum(o * d.astype(f32), 0, keepdims=True)
        o = o.T
        for i in range(8):
            att_ref[:, cols(h * 8 + i, HD)] = o[i * HD : (i + 1) * HD].astype(bf16)
        store(h, 0).start()

        @pl.when(h < 2)
        def _():
            receive(gather_one(h + 2))
            start(gather_two(h + 2) + share_one(h + 2))

        @pl.when(h > 0)
        def _():
            first_reduce(h - 1)

        @pl.when(h < 3)
        def _():
            receive(gather_two(h + 1))
            start(share_two(h + 1))

        ds = (e.astype(f32) * (dot(value, d) - delta)).astype(bf16)
        dk = dot_nt(ds, (qT[:, c].astype(f32) * inv).astype(bf16)) * (adv * SCALE)
        dv = dot_nt(e, (d.astype(f32) * inv).astype(bf16)) * adv
        for i, place_ in enumerate((2, 0, 1)):
            mine[h, place_, 0] = dk[i * TILE : (i + 1) * TILE].astype(bf16)
            mine[h, place_, 1] = dv[i * TILE : (i + 1) * TILE].astype(bf16)
        start(swap(h))
        g = (dot(key.T, ds) * (inv * (adv * SCALE))).T
        for i in range(8):
            dq_ref[:, cols(h * 8 + i, HD)] = g[i * HD : (i + 1) * HD].astype(bf16)
        store(h, 1).start()
        return carry

    lax.fori_loop(0, KVH, head, 0)

    first_reduce(3)
    second_reduce(1)
    second_reduce(2)
    receive(reduce_two(0))
    close(0)
    second_reduce(3)
    for h in (1, 2):
        receive(reduce_two(h))
        close(h)
    sent(more)
    store_adv.wait()

    def drain(h, carry):
        sent(share_one(h) + share_two(h) + swap(h) + reduce_one(h))
        pl.when(h < 3)(lambda: sent(reduce_two(h)))
        for i in range(2):
            store(h, i).wait()
        return carry

    lax.fori_loop(0, KVH, drain, 0)
    receive(reduce_two(3))
    close(3)
    stores = [
        pltpu.make_async_copy(gk_ref, gk_hbm, loc_sem.at[9]),
        pltpu.make_async_copy(gv_ref, gv_hbm, loc_sem.at[10]),
    ]
    for copy in stores:
        copy.start()
    sent(reduce_two(3))
    for copy in stores:
        copy.wait()


def finish(*refs):
    ins, outs, bufs, adv_out = refs[:5], refs[5:9], refs[10:15], refs[9]
    arrive, leave = refs[15], refs[16]
    loads, stores = [], []
    for i, pieces in enumerate((4, 4, 1, 1)):
        size = HALF // pieces
        for p in range(pieces):
            rows = pl.ds(p * size, size)
            n = len(loads)
            loads.append(pltpu.make_async_copy(ins[i].at[rows], bufs[i].at[rows], arrive.at[n]))
            stores.append(pltpu.make_async_copy(bufs[i].at[rows], outs[i].at[rows], leave.at[n]))
    last = pltpu.make_async_copy(ins[4], bufs[4], arrive.at[10])
    last.start()
    for copy in loads:
        copy.start()
    for load, copy in zip(loads, stores):
        load.wait()
        copy.start()
    last.wait()
    adv_out[0] = bufs[4][0, 0]
    for copy in stores:
        copy.wait()


def body(queries, keys, values, d_out, lengths, ancestors, rewards, pruned, branch_group):
    hbm = pl.BlockSpec(memory_space=pl.ANY)
    dma = pltpu.SemaphoreType.DMA
    wide = jax.ShapeDtypeStruct((HALF, H * HD), bf16)
    narrow = jax.ShapeDtypeStruct((HALF, KVH * HD), bf16)
    i32 = jnp.int32
    results = pl.pallas_call(
        kernel,
        out_shape=(wide, wide, narrow, narrow, jax.ShapeDtypeStruct((8, 128), f32)),
        in_specs=[hbm] * 9,
        out_specs=(hbm,) * 5,
        scratch_shapes=[
            pltpu.VMEM((HALF, H * HD), bf16),
            pltpu.VMEM((HALF, H * HD), bf16),
            pltpu.VMEM((HALF, H * HD), bf16),
            pltpu.VMEM((HALF, H * HD), bf16),
            pltpu.VMEM((HALF, KVH * HD), bf16),
            pltpu.VMEM((HALF, KVH * HD), bf16),
            pltpu.VMEM((8, 128), f32),
            pltpu.SMEM(lengths.shape, i32),
            pltpu.SMEM(ancestors.shape, i32),
            pltpu.SMEM((1,), f32),
            pltpu.SMEM((1,), i32),
            pltpu.SMEM((1,), i32),
            pltpu.VMEM((KVH, 2, 4, 2, TILE, HD), bf16),
            pltpu.VMEM((HD, H * HALF), bf16),
            pltpu.VMEM((HD, H * HALF), bf16),
            pltpu.VMEM((2, TILE, HALF), f32),
            pltpu.VMEM((8, 8, 128), f32),
            pltpu.VMEM((8, 8, 128), f32),
            pltpu.VMEM((KVH, 3, 2, TILE, HD), bf16),
            pltpu.VMEM((KVH, 2, 2, TILE, HD), bf16),
            pltpu.VMEM((KVH, 8, 2, HALF, HD), bf16),
            pltpu.VMEM((KVH, 8, 2, HALF, HD), bf16),
            dma((15,)),
            dma((32,)),
            dma((32,)),
            dma((12,)),
            dma((12,)),
            dma((8,)),
            dma((15,)),
            dma((32,)),
        ],
        compiler_params=pltpu.CompilerParams(
            collective_id=0, has_side_effects=True, vmem_limit_bytes=56 << 20
        ),
        name="tree_attention",
    )(queries, keys, values, d_out, lengths, ancestors, rewards, pruned, branch_group)
    return pl.pallas_call(
        finish,
        out_shape=(wide, wide, narrow, narrow, jax.ShapeDtypeStruct((1,), f32)),
        in_specs=[hbm] * 5,
        out_specs=(hbm,) * 4 + (pl.BlockSpec(memory_space=pltpu.SMEM),),
        scratch_shapes=[pltpu.VMEM(a.shape, a.dtype) for a in results] + [dma((11,)), dma((10,))],
        name="finish",
    )(*results)


def solution(mesh):
    rows = P(("ctx", "tp"), None)
    in_specs = (rows, rows, rows, rows, P(), P("ctx", None), P("ctx"), P("ctx"), P("ctx"))
    out_specs = (rows, rows, rows, rows, P("ctx"))
    return jax.shard_map(body, mesh=mesh, in_specs=in_specs, out_specs=out_specs, check_vma=False)
```
